256 devices in a mesh: grp: 8 (over y, x_hi), dev: 32 (over z, x_lo, core).
Axes of the slice: x: 4 (x_hi: 2, x_lo: 2; x = x_hi * 2 + x_lo), y: 4, z: 8, core: 2. Of those that a mesh axis runs over, the one named last changes fastest.
Arguments:
- train_grads: bfloat16 [4096, 8192], P(('grp', 'dev')), may hold values from -6 to 6
- query_grads: bfloat16 [8192, 128], P('dev'), may hold values from -6 to 6
Outputs:
- scores: float32 [4096, 128], P(('grp', 'dev'))
The draws below stay inside these ranges and needn't reach their ends.
All inputs are finite; a program needn't handle non-finite values.
Results may differ from the reference program's by a relative error of at most 0.0037.
Values may be sent and summed in bfloat16 or wider, within the bound.
A program may use at most 64 MiB of HBM per device.

```python
import math
import jax
import jax.numpy as jnp
from jax import lax

K = 8192
QUERIES = 128
ITERS = 2
TRAIN = 4096


def draw_train_grads(key, part):
    key = jax.random.fold_in(key, 11)
    values = jax.random.truncated_normal(key, -6.0, 6.0, (TRAIN, K), jnp.float32)
    return values.astype(jnp.bfloat16)


def levels(rng, shape, cuts, smallest, top_value):
    factor_of, own = 1.0, jax.random.fold_in(rng, 6)
    for axis_at, blocks in cuts:
        steps = jnp.exp(jax.random.uniform(jax.random.fold_in(own, axis_at), (blocks,), jnp.float32, smallest / len(cuts), top_value / len(cuts)))
        factor_of = factor_of * jnp.repeat(steps, shape[axis_at] // blocks).reshape([-1 if axis == axis_at else 1 for axis in range(len(shape))])
    return factor_of


def gaussian(key, extent, spread, most, pieces=(), held_as=jnp.bfloat16):
    drawn = spread * jax.random.normal(key, extent, jnp.float32)
    if pieces:
        drawn = drawn * levels(key, extent, pieces, -0.22, 0.18)
    return jnp.clip(drawn, -most, most).astype(held_as)


def setup_inputs(seed: int = 0) -> dict:
    key_of = jax.random.split(jax.random.key(seed), 3)
    train_grads = draw_train_grads(jax.random.fold_in(key_of[2], 71), 0)
    query_grads = gaussian(key_of[1], (K, QUERIES), 1.0, 6.0, ((0, 32),))
    return {"train_grads": train_grads, "query_grads": query_grads}


DAMP = 1.0

def step_size(width, total_rows):
    bound = (1.0 + math.sqrt(width / total_rows)) ** 2
    return 1.0 / (1.0 + 1.5 * bound)

def reference(train_grads, query_grads):
    total_rows = train_grads.shape[0]
    omega = step_size(train_grads.shape[1], total_rows)
    fisher = lax.dot_general(train_grads, train_grads, (((0,), (0,)), ((), ())), preferred_element_type=jnp.float32) / total_rows
    query = query_grads.astype(jnp.float32)
    whitened = omega * query
    for sweep in range(ITERS):
        applied = jnp.dot(fisher, whitened, precision=lax.Precision.HIGHEST)
        whitened = whitened + omega * (query - applied - DAMP * whitened)
    whitened_half = whitened.astype(jnp.bfloat16)
    return jnp.dot(train_grads, whitened_half, preferred_element_type=jnp.float32)
```

```python
import functools
import math

import jax
import jax.numpy as jnp
from jax import lax
from jax.experimental import pallas as pl
from jax.experimental.pallas import tpu as pltpu
from jax.sharding import PartitionSpec as P

ITERS = 2
DAMP = 1.0
NX = 4
MESH = pl.DeviceIdType.MESH
F32 = jnp.float32
BF16 = jnp.bfloat16


def step_size(width, total_rows):
    bound = (1.0 + math.sqrt(width / total_rows)) ** 2
    return 1.0 / (1.0 + 1.5 * bound)


def ring(d, n):
    return min(d, n - d)


def variants(packed):
    low = lax.broadcasted_iota(jnp.int32, packed.shape, 1) < 64
    wide = packed.astype(F32)
    turned = pltpu.roll(wide, 64, 1)
    zero = jnp.zeros_like(wide)
    parts = (
        jnp.where(low, wide, zero),
        jnp.where(low, turned, zero),
        jnp.where(low, zero, turned),
        jnp.where(low, zero, wide),
    )
    return [part.astype(BF16) for part in parts]


def dot(a, b):
    return jnp.dot(a, b, preferred_element_type=F32)


def kernel(
    n_grp, n_z, omega, total_rows,
    g_ref, q_ref, o_ref,
    gbuf, gt, qbuf, qpack, send_s, recv_s, sbuf, send_t, recv_t, wbuf, wlast, send_o, recv_o,
    local_sem, send_sem, g_sem, core_sem, q_sem, rs_sem, ag_sem, rt_sem, aw_sem, o_sem,
):
    rows = g_ref.shape[0]
    block = q_ref.shape[0]
    places = 2 * n_grp
    ny = places // NX
    piece = block // n_z
    grp = lax.axis_index("grp")
    dev = lax.axis_index("dev")
    z, x_lo, core = dev // 4, lax.rem(dev // 2, 2), lax.rem(dev, 2)
    place = grp * 2 + x_lo
    y, x = place // NX, lax.rem(place, NX)

    offsets = [(dy, dx) for dy in range(ny) for dx in range(NX) if (dy, dx) != (0, 0)]
    offsets.sort(key=lambda o: -(ring(o[0], ny) + ring(o[1], NX)))
    hops = sorted(range(1, n_z), key=lambda d: -ring(d, n_z))

    def place_at(offset):
        return lax.rem(y + offset[0], ny) * NX + lax.rem(x + offset[1], NX)

    def in_plane(there, c=core):
        return (there // 2, z * 4 + lax.rem(there, 2) * 2 + c)

    def z_at(d):
        return lax.rem(z + d, n_z)

    def along_z(there, c=core):
        return (grp, there * 4 + x_lo * 2 + c)

    sibling = (grp, dev + 1 - 2 * core)

    def turned(c):
        return (z, grp * 4 + x_lo * 2 + c)

    def push(src, dst, sem, to):
        copy = pltpu.make_async_remote_copy(
            src_ref=src, dst_ref=dst, send_sem=send_sem.at[0], recv_sem=sem, device_id=to, device_id_type=MESH
        )
        copy.start()

    def arrived(like, sem):
        pltpu.make_async_copy(like, like, sem).wait()

    def row_block(p, n):
        return pl.ds(pl.multiple_of(p * n, n), n)

    barrier = pltpu.get_barrier_semaphore()
    for d in hops:
        for c in (0, 1):
            pl.semaphore_signal(barrier, inc=1, device_id=along_z(z_at(d), c), device_id_type=MESH)
    for o in offsets:
        pl.semaphore_signal(barrier, inc=1, device_id=in_plane(place_at(o)), device_id_type=MESH)
    pl.semaphore_signal(barrier, inc=1, device_id=sibling, device_id_type=MESH)

    @pl.when(z != grp)
    def _():
        for c in (0, 1):
            pl.semaphore_signal(barrier, inc=1, device_id=turned(c), device_id_type=MESH)

    others = 2 * len(hops) + len(offsets) + 1
    pl.semaphore_wait(barrier, jnp.where(z != grp, others + 2, others))

    @pl.when(z != grp)
    def _():
        for c in (0, 1):
            push(q_ref, qbuf.at[core], q_sem.at[core], turned(c))

    @pl.when(z == grp)
    def _():
        push(q_ref, qbuf.at[core], q_sem.at[core], sibling)
        pltpu.make_async_copy(q_ref, qbuf.at[core], q_sem.at[core]).start()

    width = 2 * block

    def columns(p):
        return g_ref.at[:, pl.ds(pl.multiple_of(p * width, width), width)]

    mine = gbuf.at[core, row_block(place, rows)]
    own = pltpu.make_async_copy(columns(place), mine, local_sem.at[0])
    own.start()
    for o in offsets:
        there = place_at(o)
        push(columns(there), mine, g_sem.at[0], in_plane(there))
    own.wait()
    arrived(gbuf.at[0, pl.ds(0, (places - 1) * rows)], g_sem.at[0])
    push(gbuf.at[core], gbuf.at[core], core_sem.at[0], sibling)

    arrived(qbuf.at[0], q_sem.at[0])
    arrived(qbuf.at[1], q_sem.at[1])
    top, bottom = qbuf[0].astype(F32), qbuf[1].astype(F32)
    low = lax.broadcasted_iota(jnp.int32, top.shape, 1) < 64
    first = core == 0
    packed_q = jnp.where(
        low,
        jnp.where(first, top, pltpu.roll(top, 64, 1)),
        jnp.where(first, pltpu.roll(bottom, 64, 1), bottom),
    )
    qpack[...] = packed_q.astype(BF16)
    arrived(gbuf.at[0], core_sem.at[0])

    def project(packed):
        a, b, c, d = variants(packed)
        return dot(gbuf[0], jnp.concatenate([a, b], 0)) + dot(gbuf[1], jnp.concatenate([c, d], 0))

    def back(packed):
        a, b, c, d = variants(packed)
        return dot(gt[0], jnp.concatenate([a, b], 0)) + dot(gt[1], jnp.concatenate([c, d], 0))

    my_rows = row_block(place, rows)
    my_piece = row_block(z, piece)
    query = None
    whitened = None
    for sweep in range(ITERS):
        send_s[sweep] = project(qpack[...] if sweep == 0 else wbuf[...]).astype(BF16)
        for i, o in enumerate(offsets):
            there = place_at(o)
            push(send_s.at[sweep, row_block(there, rows)], recv_s.at[sweep, i], rs_sem.at[sweep], in_plane(there))
        if sweep == 0:
            top_rows = places * rows
            for half in (0, 1):
                for part in (0, 1):
                    gt[half, :, pl.ds(part * top_rows, top_rows)] = gbuf[part, :, pl.ds(half * block, block)].T
            query = qpack[my_piece, :].astype(F32)
        arrived(recv_s.at[sweep], rs_sem.at[sweep])
        total = send_s[sweep, my_rows, :].astype(F32)
        for i in range(len(offsets)):
            total = total + recv_s[sweep, i].astype(F32)
        sbuf[sweep, my_rows, :] = total.astype(BF16)
        for o in offsets:
            there = place_at(o)
            push(sbuf.at[sweep, my_rows], sbuf.at[sweep, my_rows], ag_sem.at[sweep], in_plane(there))
        arrived(sbuf.at[sweep, pl.ds(0, (places - 1) * rows)], ag_sem.at[sweep])

        send_t[sweep] = back(sbuf[sweep]).astype(BF16)
        for i, d in enumerate(hops):
            there = z_at(d)
            push(send_t.at[sweep, row_block(there, piece)], recv_t.at[sweep, i], rt_sem.at[sweep], along_z(there))
        arrived(recv_t.at[sweep], rt_sem.at[sweep])
        total = send_t[sweep, my_piece, :].astype(F32)
        for i in range(len(hops)):
            total = total + recv_t[sweep, i].astype(F32)
        applied = total * (1.0 / total_rows)
        if sweep == 0:
            applied = omega * applied
            whitened = omega * query
        whitened = whitened + omega * (query - applied - DAMP * whitened)
        if sweep < ITERS - 1:
            wbuf[my_piece, :] = whitened.astype(BF16)
            for d in hops:
                push(wbuf.at[my_piece], wbuf.at[my_piece], aw_sem.at[0], along_z(z_at(d)))
            arrived(wbuf.at[pl.ds(0, (n_z - 1) * piece)], aw_sem.at[0])
        else:
            spot = wlast.at[core, my_piece]
            wlast[core, my_piece, :] = whitened.astype(BF16)
            for d in hops:
                for c in (0, 1):
                    push(spot, spot, aw_sem.at[1 + core], along_z(z_at(d), c))
            push(spot, spot, aw_sem.at[1 + core], sibling)
            arrived(wlast.at[0, pl.ds(0, (n_z - 1) * piece)], aw_sem.at[1 + core])
            arrived(wlast.at[0], aw_sem.at[2 - core])

    left, right = wlast[0].astype(F32), wlast[1].astype(F32)
    top = jnp.where(low, left, pltpu.roll(right, 64, 1)).astype(BF16)
    bottom = jnp.where(low, pltpu.roll(left, 64, 1), right).astype(BF16)
    send_o[...] = dot(gbuf[core], jnp.concatenate([top, bottom], 0))
    for i, o in enumerate(offsets):
        there = place_at(o)
        push(send_o.at[row_block(there, rows)], recv_o.at[i], o_sem.at[0], in_plane(there))
    arrived(recv_o, o_sem.at[0])
    total = send_o[my_rows, :]
    for i in range(len(offsets)):
        total = total + recv_o[i]
    o_ref[...] = total

    sent = send_sem.at[0]

    @pl.when(z != grp)
    def _():
        arrived(qbuf, sent)

    @pl.when(z == grp)
    def _():
        arrived(qbuf.at[0], sent)

    arrived(gbuf.at[0, pl.ds(0, (places - 1) * rows)], sent)
    arrived(gbuf.at[0], sent)
    for sweep in range(ITERS):
        arrived(recv_s.at[sweep], sent)
        arrived(sbuf.at[sweep, pl.ds(0, (places - 1) * rows)], sent)
        arrived(recv_t.at[sweep], sent)
    arrived(wbuf.at[pl.ds(0, (n_z - 1) * piece)], sent)
    arrived(wlast.at[0, pl.ds(0, (n_z - 1) * piece)], sent)
    arrived(wlast.at[0], sent)
    arrived(recv_o, sent)


def body(n_grp, n_dev, train_grads, query_grads):
    rows, width = train_grads.shape
    block, queries = query_grads.shape
    n_z = n_dev // 4
    places = 2 * n_grp
    total_rows = rows * n_grp * n_dev
    piece = block // n_z
    omega = step_size(width, total_rows)
    vmem = pl.BlockSpec(memory_space=pltpu.VMEM)
    dma = pltpu.SemaphoreType.DMA
    return pl.pallas_call(
        functools.partial(kernel, n_grp, n_z, omega, total_rows),
        name="influence",
        out_shape=jax.ShapeDtypeStruct((rows, queries), F32),
        in_specs=[vmem, vmem],
        out_specs=vmem,
        scratch_shapes=[
            pltpu.VMEM((2, places * rows, 2 * block), BF16),
            pltpu.VMEM((2, block, 2 * places * rows), BF16),
            pltpu.VMEM((2, block, queries), BF16),
            pltpu.VMEM((block, queries), BF16),
            pltpu.VMEM((ITERS, places * rows, queries), BF16),
            pltpu.VMEM((ITERS, places - 1, rows, queries), BF16),
            pltpu.VMEM((ITERS, places * rows, queries), BF16),
            pltpu.VMEM((ITERS, block, queries), BF16),
            pltpu.VMEM((ITERS, n_z - 1, piece, queries), BF16),
            pltpu.VMEM((block, queries), BF16),
            pltpu.VMEM((2, block, queries), BF16),
            pltpu.VMEM((places * rows, queries), F32),
            pltpu.VMEM((places - 1, rows, queries), F32),
            dma((1,)), dma((1,)), dma((1,)), dma((1,)), dma((2,)),
            dma((ITERS,)), dma((ITERS,)), dma((ITERS,)), dma((3,)), dma((1,)),
        ],
        compiler_params=pltpu.CompilerParams(
            collective_id=0, has_side_effects=True, vmem_limit_bytes=32 * 1024 * 1024
        ),
    )(train_grads, query_grads)


def solution(mesh):
    return jax.shard_map(
        functools.partial(body, mesh.shape["grp"], mesh.shape["dev"]),
        mesh=mesh,
        in_specs=(P(("grp", "dev"), None), P("dev", None)),
        out_specs=P(("grp", "dev"), None),
        check_vma=False,
    )
```

```python
import functools
import math

import jax
import jax.numpy as jnp
from jax import lax
from jax.experimental import pallas as pl
from jax.experimental.pallas import tpu as pltpu
from jax.sharding import PartitionSpec as P

ITERS = 2
DAMP = 1.0
NX = 4
MESH = pl.DeviceIdType.MESH
F32 = jnp.float32
BF16 = jnp.bfloat16


def step_size(width, total_rows):
    bound = (1.0 + math.sqrt(width / total_rows)) ** 2
    return 1.0 / (1.0 + 1.5 * bound)


def ring(d, n):
    return min(d, n - d)


def variants(packed):
    low = lax.broadcasted_iota(jnp.int32, packed.shape, 1) < 64
    wide = packed.astype(F32)
    turned = pltpu.roll(wide, 64, 1)
    zero = jnp.zeros_like(wide)
    parts = (
        jnp.where(low, wide, zero),
        jnp.where(low, turned, zero),
        jnp.where(low, zero, turned),
        jnp.where(low, zero, wide),
    )
    return [part.astype(BF16) for part in parts]


def dot(a, b):
    return jnp.dot(a, b, preferred_element_type=F32)


def kernel(
    n_grp, n_z, omega, total_rows,
    g_ref, q_ref, o_ref,
    gl, ql, gbuf, gt, qbuf, qpack, send_s, recv_s, sbuf, send_t, recv_t, wbuf, wlast, send_o, recv_o,
    local_sem, send_sem, g_sem, core_sem, q_sem, rs_sem, ag_sem, rt_sem, aw_sem, o_sem,
):
    rows = g_ref.shape[0]
    block = q_ref.shape[0]
    places = 2 * n_grp
    ny = places // NX
    piece = block // n_z
    grp = lax.axis_index("grp")
    dev = lax.axis_index("dev")
    z, x_lo, core = dev // 4, lax.rem(dev // 2, 2), lax.rem(dev, 2)
    place = grp * 2 + x_lo
    y, x = place // NX, lax.rem(place, NX)

    offsets = [(dy, dx) for dy in range(ny) for dx in range(NX) if (dy, dx) != (0, 0)]
    offsets.sort(key=lambda o: -(ring(o[0], ny) + ring(o[1], NX)))
    hops = sorted(range(1, n_z), key=lambda d: -ring(d, n_z))

    def place_at(offset):
        return lax.rem(y + offset[0], ny) * NX + lax.rem(x + offset[1], NX)

    def in_plane(there, c=core):
        return (there // 2, z * 4 + lax.rem(there, 2) * 2 + c)

    def z_at(d):
        return lax.rem(z + d, n_z)

    def along_z(there, c=core):
        return (grp, there * 4 + x_lo * 2 + c)

    sibling = (grp, dev + 1 - 2 * core)

    def turned(c):
        return (z, grp * 4 + x_lo * 2 + c)

    leaving = []

    def push(src, dst, sem, to):
        copy = pltpu.make_async_remote_copy(
            src_ref=src, dst_ref=dst, send_sem=send_sem.at[0], recv_sem=sem, device_id=to, device_id_type=MESH
        )
        copy.start()
        leaving.append(src)

    def arrived(like, sem):
        pltpu.make_async_copy(like, like, sem).wait()

    def row_block(p, n):
        return pl.ds(pl.multiple_of(p * n, n), n)

    load_g = pltpu.make_async_copy(g_ref, gl, local_sem.at[1])
    load_q = pltpu.make_async_copy(q_ref, ql, local_sem.at[2])
    load_g.start()
    load_q.start()

    barrier = pltpu.get_barrier_semaphore()
    for d in hops:
        for c in (0, 1):
            pl.semaphore_signal(barrier, inc=1, device_id=along_z(z_at(d), c), device_id_type=MESH)
    for o in offsets:
        pl.semaphore_signal(barrier, inc=1, device_id=in_plane(place_at(o)), device_id_type=MESH)
    pl.semaphore_signal(barrier, inc=1, device_id=sibling, device_id_type=MESH)

    @pl.when(z != grp)
    def _():
        for c in (0, 1):
            pl.semaphore_signal(barrier, inc=1, device_id=turned(c), device_id_type=MESH)

    others = 2 * len(hops) + len(offsets) + 1
    pl.semaphore_wait(barrier, jnp.where(z != grp, others + 2, others))

    load_q.wait()
    load_g.wait()

    push(ql, qbuf.at[core], q_sem.at[core], turned(1 - core))

    @pl.when(z != grp)
    def _():
        push(ql, qbuf.at[core], q_sem.at[core], turned(core))

    @pl.when(z == grp)
    def _():
        pltpu.make_async_copy(ql, qbuf.at[core], q_sem.at[core]).start()

    leaving.pop()

    width = 2 * block

    def columns(p):
        return gl.at[:, pl.ds(pl.multiple_of(p * width, width), width)]

    mine = gbuf.at[core, row_block(place, rows)]
    own = pltpu.make_async_copy(columns(place), mine, local_sem.at[0])
    own.start()
    for o in offsets:
        there = place_at(o)
        push(columns(there), mine, g_sem.at[0], in_plane(there))
    own.wait()
    arrived(gbuf.at[0, pl.ds(0, (places - 1) * rows)], g_sem.at[0])
    push(gbuf.at[core], gbuf.at[core], core_sem.at[0], sibling)

    arrived(qbuf.at[0], q_sem.at[0])
    arrived(qbuf.at[1], q_sem.at[1])
    top, bottom = qbuf[0].astype(F32), qbuf[1].astype(F32)
    low = lax.broadcasted_iota(jnp.int32, top.shape, 1) < 64
    first = core == 0
    packed_q = jnp.where(
        low,
        jnp.where(first, top, pltpu.roll(top, 64, 1)),
        jnp.where(first, pltpu.roll(bottom, 64, 1), bottom),
    )
    qpack[...] = packed_q.astype(BF16)
    arrived(gbuf.at[0], core_sem.at[0])

    def project(packed):
        a, b, c, d = variants(packed)
        return dot(gbuf[0], jnp.concatenate([a, b], 0)) + dot(gbuf[1], jnp.concatenate([c, d], 0))

    def back(packed):
        a, b, c, d = variants(packed)
        return dot(gt[0], jnp.concatenate([a, b], 0)) + dot(gt[1], jnp.concatenate([c, d], 0))

    my_rows = row_block(place, rows)
    my_piece = row_block(z, piece)
    query = None
    whitened = None
    for sweep in range(ITERS):
        send_s[sweep] = project(qpack[...] if sweep == 0 else wbuf[...]).astype(BF16)
        for i, o in enumerate(offsets):
            there = place_at(o)
            push(send_s.at[sweep, row_block(there, rows)], recv_s.at[sweep, i], rs_sem.at[sweep], in_plane(there))
        if sweep == 0:
            top_rows = places * rows
            for half in (0, 1):
                for part in (0, 1):
                    gt[half, :, pl.ds(part * top_rows, top_rows)] = gbuf[part, :, pl.ds(half * block, block)].T
            query = qpack[my_piece, :].astype(F32)
        arrived(recv_s.at[sweep], rs_sem.at[sweep])
        total = send_s[sweep, my_rows, :].astype(F32)
        for i in range(len(offsets)):
            total = total + recv_s[sweep, i].astype(F32)
        sbuf[sweep, my_rows, :] = total.astype(BF16)
        for o in offsets:
            there = place_at(o)
            push(sbuf.at[sweep, my_rows], sbuf.at[sweep, my_rows], ag_sem.at[sweep], in_plane(there))
        arrived(sbuf.at[sweep, pl.ds(0, (places - 1) * rows)], ag_sem.at[sweep])

        send_t[sweep] = back(sbuf[sweep]).astype(BF16)
        for i, d in enumerate(hops):
            there = z_at(d)
            push(send_t.at[sweep, row_block(there, piece)], recv_t.at[sweep, i], rt_sem.at[sweep], along_z(there))
        arrived(recv_t.at[sweep], rt_sem.at[sweep])
        total = send_t[sweep, my_piece, :].astype(F32)
        for i in range(len(hops)):
            total = total + recv_t[sweep, i].astype(F32)
        applied = total * (1.0 / total_rows)
        if sweep == 0:
            applied = omega * applied
            whitened = omega * query
        whitened = whitened + omega * (query - applied - DAMP * whitened)
        if sweep < ITERS - 1:
            wbuf[my_piece, :] = whitened.astype(BF16)
            for d in hops:
                push(wbuf.at[my_piece], wbuf.at[my_piece], aw_sem.at[0], along_z(z_at(d)))
            arrived(wbuf.at[pl.ds(0, (n_z - 1) * piece)], aw_sem.at[0])
        else:
            spot = wlast.at[core, my_piece]
            wlast[core, my_piece, :] = whitened.astype(BF16)
            for d in hops:
                for c in (0, 1):
                    push(spot, spot, aw_sem.at[1 + core], along_z(z_at(d), c))
            push(spot, spot, aw_sem.at[1 + core], sibling)
            arrived(wlast.at[0, pl.ds(0, (n_z - 1) * piece)], aw_sem.at[1 + core])
            arrived(wlast.at[0], aw_sem.at[2 - core])

    left, right = wlast[0].astype(F32), wlast[1].astype(F32)
    top = jnp.where(low, left, pltpu.roll(right, 64, 1)).astype(BF16)
    bottom = jnp.where(low, pltpu.roll(left, 64, 1), right).astype(BF16)
    send_o[...] = dot(gbuf[core], jnp.concatenate([top, bottom], 0))
    for i, o in enumerate(offsets):
        there = place_at(o)
        push(send_o.at[row_block(there, rows)], recv_o.at[i], o_sem.at[0], in_plane(there))
    arrived(recv_o, o_sem.at[0])
    total = send_o[my_rows, :]
    for i in range(len(offsets)):
        total = total + recv_o[i]
    o_ref[...] = total

    for src in leaving:
        arrived(src, send_sem.at[0])

    @pl.when(z != grp)
    def _():
        arrived(ql, send_sem.at[0])


def body(n_grp, n_dev, train_grads, query_grads):
    rows, width = train_grads.shape
    block, queries = query_grads.shape
    n_z = n_dev // 4
    places = 2 * n_grp
    total_rows = rows * n_grp * n_dev
    piece = block // n_z
    omega = step_size(width, total_rows)
    vmem = pl.BlockSpec(memory_space=pltpu.VMEM)
    anywhere = pl.BlockSpec(memory_space=pl.ANY)
    dma = pltpu.SemaphoreType.DMA
    return pl.pallas_call(
        functools.partial(kernel, n_grp, n_z, omega, total_rows),
        name="influence",
        out_shape=jax.ShapeDtypeStruct((rows, queries), F32),
        in_specs=[anywhere, anywhere],
        out_specs=vmem,
        scratch_shapes=[
            pltpu.VMEM((rows, width), BF16),
            pltpu.VMEM((block, queries), BF16),
            pltpu.VMEM((2, places * rows, 2 * block), BF16),
            pltpu.VMEM((2, block, 2 * places * rows), BF16),
            pltpu.VMEM((2, block, queries), BF16),
            pltpu.VMEM((block, queries), BF16),
            pltpu.VMEM((ITERS, places * rows, queries), BF16),
            pltpu.VMEM((ITERS, places - 1, rows, queries), BF16),
            pltpu.VMEM((ITERS, places * rows, queries), BF16),
            pltpu.VMEM((ITERS, block, queries), BF16),
            pltpu.VMEM((ITERS, n_z - 1, piece, queries), BF16),
            pltpu.VMEM((block, queries), BF16),
            pltpu.VMEM((2, block, queries), BF16),
            pltpu.VMEM((places * rows, queries), F32),
            pltpu.VMEM((places - 1, rows, queries), F32),
            dma((3,)), dma((1,)), dma((1,)), dma((1,)), dma((2,)),
            dma((ITERS,)), dma((ITERS,)), dma((ITERS,)), dma((3,)), dma((1,)),
        ],
        compiler_params=pltpu.CompilerParams(
            collective_id=0, has_side_effects=True, vmem_limit_bytes=56 * 1024 * 1024
        ),
    )(train_grads, query_grads)


def solution(mesh):
    return jax.shard_map(
        functools.partial(body, mesh.shape["grp"], mesh.shape["dev"]),
        mesh=mesh,
        in_specs=(P(("grp", "dev"), None), P("dev", None)),
        out_specs=P(("grp", "dev"), None),
        check_vma=False,
    )
```

```python
import functools
import math

import jax
import jax.numpy as jnp
from jax import lax
from jax.experimental import pallas as pl
from jax.experimental.pallas import tpu as pltpu
from jax.sharding import PartitionSpec as P

ITERS = 2
DAMP = 1.0
NX = 4
CORES = 2
SLICES = NX * CORES
MESH = pl.DeviceIdType.MESH
F32 = jnp.float32
BF16 = jnp.bfloat16


def step_size(width, total_rows):
    bound = (1.0 + math.sqrt(width / total_rows)) ** 2
    return 1.0 / (1.0 + 1.5 * bound)


def ring(d, n):
    return min(d, n - d)


def farthest_first(n):
    return sorted(range(1, n), key=lambda d: (-ring(d, n), d))


def kernel(
    n_grp, n_z, omega, total_rows,
    g_ref, q_ref, o_ref,
    gl, ql, gbuf, qb, qt, send_s, recv_s, send_t, recv_t, wlast, send_o, recv_o,
    local_sem, send_sem, q_sem, gz_sem, gx_sem, gc_sem, s_sem, t_sem, w_sem, o_sem,
):
    rows = g_ref.shape[0]
    block = q_ref.shape[0]
    width = 4 * block
    ny = n_grp * 2 // NX
    grp = lax.axis_index("grp")
    dev = lax.axis_index("dev")
    z, x_lo, core = dev // 4, lax.rem(dev // 2, 2), lax.rem(dev, 2)
    y, x = grp // 2, lax.rem(grp, 2) * 2 + x_lo
    mine = x * CORES + core

    def device(x_at, y_at, z_at, c):
        return (y_at * 2 + x_at // 2, z_at * 4 + lax.rem(x_at, 2) * 2 + c)

    def z_at(d):
        return lax.rem(z + d, n_z)

    along_z = farthest_first(n_z)
    z_partners = [device(x, y, z_at(d), core) for d in along_z]
    x_partners = [[device(lax.rem(x + d, NX), y, z, c) for c in (core, 1 - core)] for d in farthest_first(NX)]
    y_partners = [device(x, lax.rem(y + d, ny), z, core) for d in farthest_first(ny)]
    sibling = device(x, y, z, 1 - core)
    leaving = []

    def push(src, dst, sem, to):
        copy = pltpu.make_async_remote_copy(
            src_ref=src, dst_ref=dst, send_sem=send_sem.at[0], recv_sem=sem, device_id=to, device_id_type=MESH
        )
        copy.start()
        leaving.append(src)

    def arrived(like, sem):
        pltpu.make_async_copy(like, like, sem).wait()

    def cut(p, n):
        return pl.ds(pl.multiple_of(p * n, n), n)

    load_g = pltpu.make_async_copy(g_ref, gl, local_sem.at[0])
    load_q = pltpu.make_async_copy(q_ref, ql, local_sem.at[1])
    load_g.start()
    load_q.start()

    barrier = pltpu.get_barrier_semaphore()
    partners = z_partners + [to for pair in x_partners for to in pair] + y_partners + [sibling]
    for to in partners:
        pl.semaphore_signal(barrier, inc=1, device_id=to, device_id_type=MESH)
    pl.semaphore_wait(barrier, len(partners))

    load_g.wait()
    own_g = pltpu.make_async_copy(gl.at[:, cut(z, width)], gbuf.at[z, x, core], local_sem.at[2])
    own_g.start()
    for d, to in zip(along_z, z_partners):
        push(gl.at[:, cut(z_at(d), width)], gbuf.at[z, x, core], gz_sem.at[n_z - d], to)

    load_q.wait()
    spot = qb.at[x_lo * 2 + core]
    own_q = pltpu.make_async_copy(ql, spot, local_sem.at[3])
    own_q.start()
    near = device(x + 1 - 2 * x_lo, y, z, core), device(x + 1 - 2 * x_lo, y, z, 1 - core)
    for to in (sibling, *near):
        push(ql, spot, q_sem.at[0], to)

    own_g.wait()
    order = sorted(range(n_z), key=lambda d: ring(d, n_z))
    for d in order:
        here = gbuf.at[z_at(d), x, core]
        if d:
            arrived(here, gz_sem.at[d])
        for same, _ in x_partners:
            push(here, here, gx_sem.at[d], same)
    own_q.wait()
    arrived(qb.at[pl.ds(0, 3)], q_sem.at[0])
    qt[...] = qb[...].reshape(width, qb.shape[-1]).astype(F32).T.astype(BF16)
    for d in order:
        arrived(gbuf.at[0, pl.ds(0, NX - 1), 0], gx_sem.at[d])
        here = gbuf.at[z_at(d), :, core]
        push(here, here, gc_sem.at[d], sibling)
    query_half = qt[cut(mine, qt.shape[0] // SLICES), :]
    query = query_half.astype(F32)
    for d in order:
        arrived(gbuf.at[0, :, 0], gc_sem.at[d])

    whitened = omega * query
    carried = query_half
    for sweep in range(ITERS):
        grads = gbuf[...].reshape(n_z * SLICES * rows, width)
        part = lax.dot_general(carried, grads, (((1,), (1,)), ((), ())), preferred_element_type=F32)
        send_s[sweep] = part.astype(BF16)
        for i, to in enumerate(z_partners):
            push(send_s.at[sweep], recv_s.at[sweep, i], s_sem.at[sweep], to)
        if z_partners:
            arrived(recv_s.at[sweep], s_sem.at[sweep])
        total = send_s[sweep].astype(F32)
        for i in range(len(z_partners)):
            total = total + recv_s[sweep, i].astype(F32)

        grads = gbuf[...].reshape(n_z * SLICES * rows, width)
        part = jnp.dot(total.astype(BF16), grads, preferred_element_type=F32)
        send_t[sweep] = part.astype(BF16)
        for i, to in enumerate(y_partners):
            push(send_t.at[sweep], recv_t.at[sweep, i], t_sem.at[sweep], to)
        if y_partners:
            arrived(recv_t.at[sweep], t_sem.at[sweep])
        total = send_t[sweep].astype(F32)
        for i in range(len(y_partners)):
            total = total + recv_t[sweep, i].astype(F32)
        applied = total * (1.0 / total_rows)
        if sweep == 0:
            applied = omega * applied
        whitened = whitened + omega * (query - applied - DAMP * whitened)
        carried = whitened.astype(BF16)

    wlast[mine] = carried
    spot = wlast.at[mine]
    for pair in x_partners:
        for to in pair:
            push(spot, spot, w_sem.at[0], to)
    push(spot, spot, w_sem.at[0], sibling)
    arrived(wlast.at[pl.ds(0, SLICES - 1)], w_sem.at[0])
    queries = wlast[...].reshape(qt.shape[0], width)
    grads = gbuf[:, x, core].reshape(n_z * rows, width)
    part = lax.dot_general(grads, queries, (((1,), (1,)), ((), ())), preferred_element_type=F32)
    send_o[...] = part.reshape(send_o.shape)
    for i, (d, to) in enumerate(zip(along_z, z_partners)):
        push(send_o.at[z_at(d)], recv_o.at[i], o_sem.at[0], to)
    if z_partners:
        arrived(recv_o, o_sem.at[0])
    total = send_o[z]
    for i in range(len(z_partners)):
        total = total + recv_o[i]
    o_ref[...] = total

    for src in leaving:
        arrived(src, send_sem.at[0])


def body(n_grp, n_dev, train_grads, query_grads):
    rows, width = train_grads.shape
    block, queries = query_grads.shape
    n_z = n_dev // 4
    ny = n_grp * 2 // NX
    total_rows = rows * n_grp * n_dev
    omega = step_size(width, total_rows)
    slice_q = queries // SLICES
    held = 4 * block
    others_z, others_y = max(n_z - 1, 1), max(ny - 1, 1)
    vmem = pl.BlockSpec(memory_space=pltpu.VMEM)
    anywhere = pl.BlockSpec(memory_space=pl.ANY)
    dma = pltpu.SemaphoreType.DMA
    return pl.pallas_call(
        functools.partial(kernel, n_grp, n_z, omega, total_rows),
        name="influence",
        out_shape=jax.ShapeDtypeStruct((rows, queries), F32),
        in_specs=[anywhere, anywhere],
        out_specs=vmem,
        scratch_shapes=[
            pltpu.VMEM((rows, width), BF16),
            pltpu.VMEM((block, queries), BF16),
            pltpu.VMEM((n_z, NX, CORES, rows, held), BF16),
            pltpu.VMEM((4, block, queries), BF16),
            pltpu.VMEM((queries, held), BF16),
            pltpu.VMEM((ITERS, slice_q, n_z * SLICES * rows), BF16),
            pltpu.VMEM((ITERS, others_z, slice_q, n_z * SLICES * rows), BF16),
            pltpu.VMEM((ITERS, slice_q, held), BF16),
            pltpu.VMEM((ITERS, others_y, slice_q, held), BF16),
            pltpu.VMEM((SLICES, slice_q, held), BF16),
            pltpu.VMEM((n_z, rows, queries), F32),
            pltpu.VMEM((others_z, rows, queries), F32),
            dma((4,)), dma((1,)), dma((1,)), dma((n_z,)), dma((n_z,)), dma((n_z,)),
            dma((ITERS,)), dma((ITERS,)), dma((1,)), dma((1,)),
        ],
        compiler_params=pltpu.CompilerParams(
            collective_id=0, has_side_effects=True, vmem_limit_bytes=56 * 1024 * 1024
        ),
    )(train_grads, query_grads)


def solution(mesh):
    return jax.shard_map(
        functools.partial(body, mesh.shape["grp"], mesh.shape["dev"]),
        mesh=mesh,
        in_specs=(P(("grp", "dev"), None), P("dev", None)),
        out_specs=P(("grp", "dev"), None),
        check_vma=False,
    )
```

```python
import functools
import math

import jax
import jax.numpy as jnp
from jax import lax
from jax.experimental import pallas as pl
from jax.experimental.pallas import tpu as pltpu
from jax.sharding import PartitionSpec as P

ITERS = 2
DAMP = 1.0
NX = 4
CORES = 2
SLICES = NX * CORES
MESH = pl.DeviceIdType.MESH
F32 = jnp.float32
BF16 = jnp.bfloat16


def step_size(width, total_rows):
    bound = (1.0 + math.sqrt(width / total_rows)) ** 2
    return 1.0 / (1.0 + 1.5 * bound)


def ring(d, n):
    return min(d, n - d)


def farthest_first(n):
    return sorted(range(1, n), key=lambda d: (-ring(d, n), d))


def dot_t(a, b):
    return lax.dot_general(a, b, (((1,), (1,)), ((), ())), preferred_element_type=F32)


def kernel(
    n_grp, n_z, omega, total_rows,
    g_ref, q_ref, o_ref,
    gl, ql, gbuf, qb, qt, send_f, recv_f, sums, first, send_s, recv_s, send_t, recv_t, send_o, recv_o, last, turned,
    local_sem, send_sem, q_sem, gz_sem, gx_sem, gc_sem, f_sem, e_sem, s_sem, t_sem, o_sem, w_sem,
):
    rows = g_ref.shape[0]
    block = q_ref.shape[0]
    width = 4 * block
    ny = n_grp * 2 // NX
    grp = lax.axis_index("grp")
    dev = lax.axis_index("dev")
    z, x_lo, core = dev // 4, lax.rem(dev // 2, 2), lax.rem(dev, 2)
    y, x = grp // 2, lax.rem(grp, 2) * 2 + x_lo
    mine = x * CORES + core

    def device(x_at, y_at, z_at, c):
        return (y_at * 2 + x_at // 2, z_at * 4 + lax.rem(x_at, 2) * 2 + c)

    def z_at(d):
        return lax.rem(z + d, n_z)

    along_z = farthest_first(n_z)
    z_partners = [device(x, y, z_at(d), core) for d in along_z]
    x_partners = [[device(lax.rem(x + d, NX), y, z, c) for c in (core, 1 - core)] for d in farthest_first(NX)]
    slice_partners = []
    for d in farthest_first(NX):
        there = lax.rem(x + d, NX)
        for c in (core, 1 - core):
            slice_partners.append((there * CORES + c, device(there, y, z, c)))
    slice_partners.append((x * CORES + 1 - core, device(x, y, z, 1 - core)))
    y_partners = [device(x, lax.rem(y + d, ny), z, core) for d in farthest_first(ny)]
    sibling = device(x, y, z, 1 - core)
    leaving = []

    def push(src, dst, sem, to):
        copy = pltpu.make_async_remote_copy(
            src_ref=src, dst_ref=dst, send_sem=send_sem.at[0], recv_sem=sem, device_id=to, device_id_type=MESH
        )
        copy.start()
        leaving.append(src)

    def arrived(like, sem):
        pltpu.make_async_copy(like, like, sem).wait()

    def cut(p, n):
        return pl.ds(pl.multiple_of(p * n, n), n)

    load_g = pltpu.make_async_copy(g_ref, gl, local_sem.at[0])
    load_q = pltpu.make_async_copy(q_ref, ql, local_sem.at[1])
    load_g.start()
    load_q.start()

    barrier = pltpu.get_barrier_semaphore()
    partners = z_partners + [to for pair in x_partners for to in pair] + y_partners + [sibling]
    for to in partners:
        pl.semaphore_signal(barrier, inc=1, device_id=to, device_id_type=MESH)
    pl.semaphore_wait(barrier, len(partners))

    load_g.wait()
    own_g = pltpu.make_async_copy(gl.at[:, cut(z, width)], gbuf.at[mine, z], local_sem.at[2])
    own_g.start()
    for d, to in reversed(list(zip(along_z, z_partners))):
        push(gl.at[:, cut(z_at(d), width)], gbuf.at[mine, z], gz_sem.at[n_z - d], to)

    load_q.wait()
    spot = qb.at[x_lo * 2 + core]
    own_q = pltpu.make_async_copy(ql, spot, local_sem.at[3])
    own_q.start()
    near = device(x + 1 - 2 * x_lo, y, z, core), device(x + 1 - 2 * x_lo, y, z, 1 - core)
    for to in (sibling, *near):
        push(ql, spot, q_sem.at[0], to)

    own_g.wait()
    order = [0] + along_z[::-1]
    for d in order:
        here = gbuf.at[mine, z_at(d)]
        if d:
            arrived(here, gz_sem.at[d])
        for same, _ in x_partners:
            push(here, here, gx_sem.at[d], same)
        if d == 0:
            own_q.wait()
            arrived(qb.at[pl.ds(0, 3)], q_sem.at[0])
            qt[...] = qb[...].reshape(width, qb.shape[-1]).astype(F32).T.astype(BF16)

    grads = gbuf[mine].reshape(n_z * rows, width)
    send_f[...] = dot_t(qt[...], grads).astype(BF16)
    for i, to in enumerate(z_partners):
        push(send_f, recv_f.at[i], f_sem.at[0], to)
    for d in order:
        arrived(gbuf.at[pl.ds(0, NX - 1), 0], gx_sem.at[d])
        for there in range(NX):
            here = gbuf.at[there * CORES + core, z_at(d)]
            push(here, here, gc_sem.at[0], sibling)
    if z_partners:
        arrived(recv_f, f_sem.at[0])
    total = send_f[...].astype(F32)
    for i in range(len(z_partners)):
        total = total + recv_f[i].astype(F32)
    sums[...] = total.astype(BF16).reshape(sums.shape)
    own_s = pltpu.make_async_copy(sums.at[mine], first.at[mine], local_sem.at[4])
    own_s.start()
    for there, to in slice_partners:
        push(sums.at[there], first.at[mine], e_sem.at[0], to)
    own_s.wait()
    arrived(first.at[pl.ds(0, SLICES - 1)], e_sem.at[0])
    carried = jnp.concatenate([first[j] for j in range(SLICES)], axis=1)
    arrived(gbuf.at[pl.ds(0, NX)], gc_sem.at[0])

    query = qt[cut(mine, qt.shape[0] // SLICES), :].astype(F32)
    whitened = omega * query
    for sweep in range(ITERS):
        if sweep:
            grads = gbuf[...].reshape(SLICES * n_z * rows, width)
            send_s[...] = dot_t(whitened.astype(BF16), grads).astype(BF16)
            for i, to in enumerate(z_partners):
                push(send_s, recv_s.at[i], s_sem.at[0], to)
            if z_partners:
                arrived(recv_s, s_sem.at[0])
            total = send_s[...].astype(F32)
            for i in range(len(z_partners)):
                total = total + recv_s[i].astype(F32)
            carried = total.astype(BF16)

        grads = gbuf[...].reshape(SLICES * n_z * rows, width)
        part = jnp.dot(carried, grads, preferred_element_type=F32)
        send_t[sweep] = part.astype(BF16)
        for i, to in enumerate(y_partners):
            push(send_t.at[sweep], recv_t.at[sweep, i], t_sem.at[sweep], to)
        if y_partners:
            arrived(recv_t.at[sweep], t_sem.at[sweep])
        total = send_t[sweep].astype(F32)
        for i in range(len(y_partners)):
            total = total + recv_t[sweep, i].astype(F32)
        applied = total * (1.0 / total_rows)
        if sweep == 0:
            applied = omega * applied
        whitened = whitened + omega * (query - applied - DAMP * whitened)

    half = whitened.astype(BF16)
    for there in range(n_z):
        grads = gbuf[:, there].reshape(SLICES * rows, width)
        send_o[there] = dot_t(half, grads)
    for i, (d, to) in enumerate(zip(along_z, z_partners)):
        push(send_o.at[z_at(d)], recv_o.at[i], o_sem.at[0], to)
    if z_partners:
        arrived(recv_o, o_sem.at[0])
    total = send_o[z]
    for i in range(len(z_partners)):
        total = total + recv_o[i]
    last[mine] = total
    for _, to in slice_partners:
        push(last.at[mine], last.at[mine], w_sem.at[0], to)
    arrived(last.at[pl.ds(0, SLICES - 1)], w_sem.at[0])
    turned[...] = last[...].reshape(qt.shape[0], SLICES * rows).T
    o_ref[...] = turned[cut(mine, rows), :]

    for src in leaving:
        arrived(src, send_sem.at[0])


def body(n_grp, n_dev, train_grads, query_grads):
    rows, width = train_grads.shape
    block, queries = query_grads.shape
    n_z = n_dev // 4
    ny = n_grp * 2 // NX
    total_rows = rows * n_grp * n_dev
    omega = step_size(width, total_rows)
    slice_q = queries // SLICES
    held = 4 * block
    others_z, others_y = max(n_z - 1, 1), max(ny - 1, 1)
    vmem = pl.BlockSpec(memory_space=pltpu.VMEM)
    anywhere = pl.BlockSpec(memory_space=pl.ANY)
    dma = pltpu.SemaphoreType.DMA
    return pl.pallas_call(
        functools.partial(kernel, n_grp, n_z, omega, total_rows),
        name="influence",
        out_shape=jax.ShapeDtypeStruct((rows, queries), F32),
        in_specs=[anywhere, anywhere],
        out_specs=vmem,
        scratch_shapes=[
            pltpu.VMEM((rows, width), BF16),
            pltpu.VMEM((block, queries), BF16),
            pltpu.VMEM((SLICES, n_z, rows, held), BF16),
            pltpu.VMEM((4, block, queries), BF16),
            pltpu.VMEM((queries, held), BF16),
            pltpu.VMEM((queries, n_z * rows), BF16),
            pltpu.VMEM((others_z, queries, n_z * rows), BF16),
            pltpu.VMEM((SLICES, slice_q, n_z * rows), BF16),
            pltpu.VMEM((SLICES, slice_q, n_z * rows), BF16),
            pltpu.VMEM((slice_q, SLICES * n_z * rows), BF16),
            pltpu.VMEM((others_z, slice_q, SLICES * n_z * rows), BF16),
            pltpu.VMEM((ITERS, slice_q, held), BF16),
            pltpu.VMEM((ITERS, others_y, slice_q, held), BF16),
            pltpu.VMEM((n_z, slice_q, SLICES * rows), F32),
            pltpu.VMEM((others_z, slice_q, SLICES * rows), F32),
            pltpu.VMEM((SLICES, slice_q, SLICES * rows), F32),
            pltpu.VMEM((SLICES * rows, queries), F32),
            dma((5,)), dma((1,)), dma((1,)), dma((n_z,)), dma((n_z,)), dma((1,)),
            dma((1,)), dma((1,)), dma((1,)), dma((ITERS,)), dma((1,)), dma((1,)),
        ],
        compiler_params=pltpu.CompilerParams(
            collective_id=0, has_side_effects=True, vmem_limit_bytes=56 * 1024 * 1024
        ),
    )(train_grads, query_grads)


def solution(mesh):
    return jax.shard_map(
        functools.partial(body, mesh.shape["grp"], mesh.shape["dev"]),
        mesh=mesh,
        in_specs=(P(("grp", "dev"), None), P("dev", None)),
        out_specs=P(("grp", "dev"), None),
        check_vma=False,
    )
```

```python
import functools
import math

import jax
import jax.numpy as jnp
from jax import lax
from jax.experimental import pallas as pl
from jax.experimental.pallas import tpu as pltpu
from jax.sharding import PartitionSpec as P

ITERS = 2
DAMP = 1.0
NX = 4
CORES = 2
SLICES = NX * CORES
MESH = pl.DeviceIdType.MESH
F32 = jnp.float32
BF16 = jnp.bfloat16


def step_size(width, total_rows):
    bound = (1.0 + math.sqrt(width / total_rows)) ** 2
    return 1.0 / (1.0 + 1.5 * bound)


def ring(d, n):
    return min(d, n - d)


def farthest_first(n):
    return sorted(range(1, n), key=lambda d: (-ring(d, n), d))


def dot_t(a, b):
    return lax.dot_general(a, b, (((1,), (1,)), ((), ())), preferred_element_type=F32)


def kernel(
    n_grp, n_z, omega, total_rows,
    g_ref, q_ref, o_ref,
    gl, ql, gbuf, qb, qt, send_f, recv_f, column, sums, first, send_s, recv_s, send_t, recv_t, send_o, recv_o, last, turned,
    local_sem, send_sem, q_sem, gz_sem, gx_sem, gc_sem, f_sem, c_sem, e_sem, s_sem, t_sem, o_sem, w_sem,
):
    rows = g_ref.shape[0]
    block = q_ref.shape[0]
    width = 4 * block
    ny = n_grp * 2 // NX
    grp = lax.axis_index("grp")
    dev = lax.axis_index("dev")
    z, x_lo, core = dev // 4, lax.rem(dev // 2, 2), lax.rem(dev, 2)
    y, x = grp // 2, lax.rem(grp, 2) * 2 + x_lo
    mine = x * CORES + core

    def device(x_at, y_at, z_at, c):
        return (y_at * 2 + x_at // 2, z_at * 4 + lax.rem(x_at, 2) * 2 + c)

    def z_at(d):
        return lax.rem(z + d, n_z)

    along_z = farthest_first(n_z)
    z_partners = [device(x, y, z_at(d), core) for d in along_z]
    x_partners = [[device(lax.rem(x + d, NX), y, z, c) for c in (core, 1 - core)] for d in farthest_first(NX)]
    slice_partners = []
    for d in farthest_first(NX):
        there = lax.rem(x + d, NX)
        for c in (core, 1 - core):
            slice_partners.append((there * CORES + c, device(there, y, z, c)))
    slice_partners.append((x * CORES + 1 - core, device(x, y, z, 1 - core)))
    y_partners = [device(x, lax.rem(y + d, ny), z, core) for d in farthest_first(ny)]
    sibling = device(x, y, z, 1 - core)
    leaving = []

    def push(src, dst, sem, to):
        copy = pltpu.make_async_remote_copy(
            src_ref=src, dst_ref=dst, send_sem=send_sem.at[0], recv_sem=sem, device_id=to, device_id_type=MESH
        )
        copy.start()
        leaving.append(math.prod(src.shape) * src.dtype.itemsize)

    def arrived(like, sem):
        pltpu.make_async_copy(like, like, sem).wait()

    def depart():
        left = sum(leaving)
        leaving.clear()
        for like in (gbuf.at[0], gbuf.at[0, 0, 0], sums.at[0]):
            size = math.prod(like.shape) * like.dtype.itemsize
            while left >= size:
                arrived(like, send_sem.at[0])
                left -= size
        assert left == 0

    def cut(p, n):
        return pl.ds(pl.multiple_of(p * n, n), n)

    load_g = pltpu.make_async_copy(g_ref, gl, local_sem.at[0])
    load_q = pltpu.make_async_copy(q_ref, ql, local_sem.at[1])
    load_g.start()
    load_q.start()

    barrier = pltpu.get_barrier_semaphore()
    partners = z_partners + [to for pair in x_partners for to in pair] + y_partners + [sibling]
    for to in partners:
        pl.semaphore_signal(barrier, inc=1, device_id=to, device_id_type=MESH)
    pl.semaphore_wait(barrier, len(partners))

    load_g.wait()
    own_g = pltpu.make_async_copy(gl.at[:, cut(z, width)], gbuf.at[x, core, z], local_sem.at[2])
    own_g.start()
    near_first = along_z[::-1]
    half_way = [d for d in near_first if 2 * d == n_z]
    for d in half_way + [d for d in near_first if 2 * d != n_z]:
        push(gl.at[:, cut(z_at(d), width)], gbuf.at[x, core, z], gz_sem.at[n_z - d], device(x, y, z_at(d), core))

    load_q.wait()
    spot = qb.at[x_lo * 2 + core]
    own_q = pltpu.make_async_copy(ql, spot, local_sem.at[3])
    own_q.start()
    near = device(x + 1 - 2 * x_lo, y, z, core), device(x + 1 - 2 * x_lo, y, z, 1 - core)
    for to in (sibling, *near):
        push(ql, spot, q_sem.at[0], to)

    groups = [[0]] + [[d for d in near_first if ring(d, n_z) == far] for far in range(1, n_z // 2 + 1)]
    if len(groups) > 3:
        groups[-2:] = groups[:-3:-1]
    own_g.wait()
    for group in groups:
        for d in group:
            here = gbuf.at[x, core, z_at(d)]
            if d:
                arrived(here, gz_sem.at[d])
            for same, _ in x_partners:
                push(here, here, gx_sem.at[d], same)
        if group == [0]:
            own_q.wait()
            arrived(qb.at[pl.ds(0, 3)], q_sem.at[0])
        pieces = [gbuf[x, core, z_at(d)] for d in group]
        pieces = pieces[0] if len(pieces) == 1 else jnp.concatenate(pieces, axis=0)
        part = jnp.dot(pieces, qb[...].reshape(width, qb.shape[-1]), preferred_element_type=F32).astype(BF16)
        for i, d in enumerate(group):
            send_f[d] = part[i * rows : (i + 1) * rows]
            if d:
                push(send_f.at[d], recv_f.at[d - 1], f_sem.at[0], device(x, y, z_at(d), core))
    qt[...] = qb[...].reshape(width, qb.shape[-1]).astype(F32).T.astype(BF16)
    if z_partners:
        arrived(recv_f, f_sem.at[0])
    total = send_f[0].astype(F32)
    for i in range(len(z_partners)):
        total = total + recv_f[i].astype(F32)
    column[z] = total.astype(BF16)
    for to in z_partners:
        push(column.at[z], column.at[z], c_sem.at[0], to)

    def across(groups):
        for group in groups:
            for d in group:
                arrived(gbuf.at[pl.ds(0, NX - 1), 0, 0], gx_sem.at[d])
                here = gbuf.at[:, core, z_at(d)]
                push(here, here, gc_sem.at[0], sibling)

    across(groups[:-1])
    if z_partners:
        arrived(column.at[pl.ds(0, n_z - 1)], c_sem.at[0])
    total = column[...].reshape(n_z * rows, qb.shape[-1]).astype(F32).T
    sums[...] = total.astype(BF16).reshape(sums.shape)
    own_s = pltpu.make_async_copy(sums.at[mine], first.at[mine], local_sem.at[4])
    own_s.start()
    for there, to in slice_partners:
        push(sums.at[there], first.at[mine], e_sem.at[0], to)
    across(groups[-1:])
    own_s.wait()
    arrived(first.at[pl.ds(0, SLICES - 1)], e_sem.at[0])
    carried = jnp.concatenate([first[j] for j in range(SLICES)], axis=1)
    arrived(gbuf.at[:, 0], gc_sem.at[0])

    query = qt[cut(mine, qt.shape[0] // SLICES), :].astype(F32)
    whitened = omega * query
    for sweep in range(ITERS):
        if sweep:
            grads = gbuf[...].reshape(SLICES * n_z * rows, width)
            send_s[...] = dot_t(whitened.astype(BF16), grads).astype(BF16)
            for i, to in enumerate(z_partners):
                push(send_s, recv_s.at[i], s_sem.at[0], to)
            if z_partners:
                arrived(recv_s, s_sem.at[0])
            total = send_s[...].astype(F32)
            for i in range(len(z_partners)):
                total = total + recv_s[i].astype(F32)
            carried = total.astype(BF16)

        grads = gbuf[...].reshape(SLICES * n_z * rows, width)
        part = jnp.dot(carried, grads, preferred_element_type=F32)
        send_t[sweep] = part.astype(BF16)
        for i, to in enumerate(y_partners):
            push(send_t.at[sweep], recv_t.at[sweep, i], t_sem.at[sweep], to)
        if y_partners:
            arrived(recv_t.at[sweep], t_sem.at[sweep])
        total = send_t[sweep].astype(F32)
        for i in range(len(y_partners)):
            total = total + recv_t[sweep, i].astype(F32)
        applied = total * (1.0 / total_rows)
        if sweep == 0:
            applied = omega * applied
        whitened = whitened + omega * (query - applied - DAMP * whitened)

    half = whitened.astype(BF16)
    for there in range(n_z):
        grads = gbuf[:, :, there].reshape(SLICES * rows, width)
        send_o[there] = dot_t(half, grads)
    for i, (d, to) in enumerate(zip(along_z, z_partners)):
        push(send_o.at[z_at(d)], recv_o.at[i], o_sem.at[0], to)
    if z_partners:
        arrived(recv_o, o_sem.at[0])
    total = send_o[z]
    for i in range(len(z_partners)):
        total = total + recv_o[i]
    last[mine] = total
    depart()
    for _, to in slice_partners:
        push(last.at[mine], last.at[mine], w_sem.at[0], to)
    arrived(last.at[pl.ds(0, SLICES - 1)], w_sem.at[0])
    turned[...] = last[...].reshape(qt.shape[0], SLICES * rows).T
    o_ref[...] = turned[cut(mine, rows), :]

    depart()


def body(n_grp, n_dev, train_grads, query_grads):
    rows, width = train_grads.shape
    block, queries = query_grads.shape
    n_z = n_dev // 4
    ny = n_grp * 2 // NX
    total_rows = rows * n_grp * n_dev
    omega = step_size(width, total_rows)
    slice_q = queries // SLICES
    held = 4 * block
    others_z, others_y = max(n_z - 1, 1), max(ny - 1, 1)
    vmem = pl.BlockSpec(memory_space=pltpu.VMEM)
    anywhere = pl.BlockSpec(memory_space=pl.ANY)
    dma = pltpu.SemaphoreType.DMA
    return pl.pallas_call(
        functools.partial(kernel, n_grp, n_z, omega, total_rows),
        name="influence",
        out_shape=jax.ShapeDtypeStruct((rows, queries), F32),
        in_specs=[anywhere, anywhere],
        out_specs=vmem,
        scratch_shapes=[
            pltpu.VMEM((rows, width), BF16),
            pltpu.VMEM((block, queries), BF16),
            pltpu.VMEM((NX, CORES, n_z, rows, held), BF16),
            pltpu.VMEM((4, block, queries), BF16),
            pltpu.VMEM((queries, held), BF16),
            pltpu.VMEM((n_z, rows, queries), BF16),
            pltpu.VMEM((others_z, rows, queries), BF16),
            pltpu.VMEM((n_z, rows, queries), BF16),
            pltpu.VMEM((SLICES, slice_q, n_z * rows), BF16),
            pltpu.VMEM((SLICES, slice_q, n_z * rows), BF16),
            pltpu.VMEM((slice_q, SLICES * n_z * rows), BF16),
            pltpu.VMEM((others_z, slice_q, SLICES * n_z * rows), BF16),
            pltpu.VMEM((ITERS, slice_q, held), BF16),
            pltpu.VMEM((ITERS, others_y, slice_q, held), BF16),
            pltpu.VMEM((n_z, slice_q, SLICES * rows), F32),
            pltpu.VMEM((others_z, slice_q, SLICES * rows), F32),
            pltpu.VMEM((SLICES, slice_q, SLICES * rows), F32),
            pltpu.VMEM((SLICES * rows, queries), F32),
            dma((5,)), dma((1,)), dma((1,)), dma((n_z,)), dma((n_z,)), dma((1,)),
            dma((1,)), dma((1,)), dma((1,)), dma((1,)), dma((ITERS,)), dma((1,)), dma((1,)),
        ],
        compiler_params=pltpu.CompilerParams(
            collective_id=0, has_side_effects=True, vmem_limit_bytes=55168 * 1024
        ),
    )(train_grads, query_grads)


def solution(mesh):
    return jax.shard_map(
        functools.partial(body, mesh.shape["grp"], mesh.shape["dev"]),
        mesh=mesh,
        in_specs=(P(("grp", "dev"), None), P("dev", None)),
        out_specs=P(("grp", "dev"), None),
        check_vma=False,
    )
```

```python
import functools
import math

import jax
import jax.numpy as jnp
from jax import lax
from jax.experimental import pallas as pl
from jax.experimental.pallas import tpu as pltpu
from jax.sharding import PartitionSpec as P

ITERS = 2
DAMP = 1.0
NX = 4
CORES = 2
SLICES = NX * CORES
MESH = pl.DeviceIdType.MESH
F32 = jnp.float32
BF16 = jnp.bfloat16


def step_size(width, total_rows):
    bound = (1.0 + math.sqrt(width / total_rows)) ** 2
    return 1.0 / (1.0 + 1.5 * bound)


def ring(d, n):
    return min(d, n - d)


def farthest_first(n):
    return sorted(range(1, n), key=lambda d: (-ring(d, n), d))


def dot_t(a, b):
    return lax.dot_general(a, b, (((1,), (1,)), ((), ())), preferred_element_type=F32)


def kernel(
    n_grp, n_z, omega, total_rows,
    g_ref, q_ref, o_ref,
    gl, ql, gbuf, qb, qt, send_f, recv_f, column, sums, first, send_s, recv_s, send_t, recv_t, send_o, recv_o, last, turned,
    local_sem, send_sem, q_sem, gz_sem, gx_sem, gc_sem, f_sem, c_sem, e_sem, s_sem, t_sem, o_sem, w_sem,
):
    rows = g_ref.shape[0]
    block = q_ref.shape[0]
    width = 4 * block
    ny = n_grp * 2 // NX
    grp = lax.axis_index("grp")
    dev = lax.axis_index("dev")
    z, x_lo, core = dev // 4, lax.rem(dev // 2, 2), lax.rem(dev, 2)
    y, x = grp // 2, lax.rem(grp, 2) * 2 + x_lo
    mine = x * CORES + core

    def device(x_at, y_at, z_at, c):
        return (y_at * 2 + x_at // 2, z_at * 4 + lax.rem(x_at, 2) * 2 + c)

    def z_at(d):
        return lax.rem(z + d, n_z)

    along_z = farthest_first(n_z)
    z_partners = [device(x, y, z_at(d), core) for d in along_z]
    x_partners = [[device(lax.rem(x + d, NX), y, z, c) for c in (core, 1 - core)] for d in farthest_first(NX)]
    slice_partners = []
    for d in farthest_first(NX):
        there = lax.rem(x + d, NX)
        for c in (core, 1 - core):
            slice_partners.append((there * CORES + c, device(there, y, z, c)))
    slice_partners.append((x * CORES + 1 - core, device(x, y, z, 1 - core)))
    y_partners = [device(x, lax.rem(y + d, ny), z, core) for d in farthest_first(ny)]
    sibling = device(x, y, z, 1 - core)
    leaving = []

    def push(src, dst, sem, to):
        copy = pltpu.make_async_remote_copy(
            src_ref=src, dst_ref=dst, send_sem=send_sem.at[0], recv_sem=sem, device_id=to, device_id_type=MESH
        )
        copy.start()
        leaving.append(math.prod(src.shape) * src.dtype.itemsize)

    def arrived(like, sem):
        pltpu.make_async_copy(like, like, sem).wait()

    def depart():
        left = sum(leaving)
        leaving.clear()
        for like in (gbuf.at[0], gbuf.at[0, 0, 0], sums.at[0]):
            size = math.prod(like.shape) * like.dtype.itemsize
            while left >= size:
                arrived(like, send_sem.at[0])
                left -= size
        assert left == 0

    def cut(p, n):
        return pl.ds(pl.multiple_of(p * n, n), n)

    load_g = pltpu.make_async_copy(g_ref, gl, local_sem.at[0])
    load_q = pltpu.make_async_copy(q_ref, ql, local_sem.at[1])
    load_g.start()
    load_q.start()

    barrier = pltpu.get_barrier_semaphore()
    partners = z_partners + [to for pair in x_partners for to in pair] + y_partners + [sibling]
    for to in partners:
        pl.semaphore_signal(barrier, inc=1, device_id=to, device_id_type=MESH)
    pl.semaphore_wait(barrier, len(partners))

    load_g.wait()
    own_g = pltpu.make_async_copy(gl.at[:, cut(z, width)], gbuf.at[x, core, z], local_sem.at[2])
    own_g.start()
    for d, to in zip(along_z, z_partners):
        push(gl.at[:, cut(z_at(d), width)], gbuf.at[x, core, z], gz_sem.at[n_z - d], to)

    load_q.wait()
    spot = qb.at[x_lo * 2 + core]
    own_q = pltpu.make_async_copy(ql, spot, local_sem.at[3])
    own_q.start()
    near = device(x + 1 - 2 * x_lo, y, z, core), device(x + 1 - 2 * x_lo, y, z, 1 - core)
    for to in (sibling, *near):
        push(ql, spot, q_sem.at[0], to)

    groups = [[0]] + [[d for d in along_z if ring(d, n_z) == far] for far in range(n_z // 2, 0, -1)]
    own_g.wait()
    for group in groups:
        for d in group:
            here = gbuf.at[x, core, z_at(d)]
            if d:
                arrived(here, gz_sem.at[d])
            for same, _ in x_partners:
                push(here, here, gx_sem.at[d], same)
        if group == [0]:
            own_q.wait()
            arrived(qb.at[pl.ds(0, 3)], q_sem.at[0])
        pieces = [gbuf[x, core, z_at(d)] for d in group]
        pieces = pieces[0] if len(pieces) == 1 else jnp.concatenate(pieces, axis=0)
        part = jnp.dot(pieces, qb[...].reshape(width, qb.shape[-1]), preferred_element_type=F32).astype(BF16)
        for i, d in enumerate(group):
            send_f[d] = part[i * rows : (i + 1) * rows]
            if d:
                push(send_f.at[d], recv_f.at[d - 1], f_sem.at[0], device(x, y, z_at(d), core))
    qt[...] = qb[...].reshape(width, qb.shape[-1]).astype(F32).T.astype(BF16)
    if z_partners:
        arrived(recv_f, f_sem.at[0])
    total = send_f[0].astype(F32)
    for i in range(len(z_partners)):
        total = total + recv_f[i].astype(F32)
    column[z] = total.astype(BF16)
    for to in z_partners:
        push(column.at[z], column.at[z], c_sem.at[0], to)

    def across(groups):
        for group in groups:
            for d in group:
                arrived(gbuf.at[pl.ds(0, NX - 1), 0, 0], gx_sem.at[d])
                here = gbuf.at[:, core, z_at(d)]
                push(here, here, gc_sem.at[0], sibling)

    across(groups[:-1])
    if z_partners:
        arrived(column.at[pl.ds(0, n_z - 1)], c_sem.at[0])
    total = column[...].reshape(n_z * rows, qb.shape[-1]).astype(F32).T
    sums[...] = total.astype(BF16).reshape(sums.shape)
    own_s = pltpu.make_async_copy(sums.at[mine], first.at[mine], local_sem.at[4])
    own_s.start()
    for there, to in slice_partners:
        push(sums.at[there], first.at[mine], e_sem.at[0], to)
    across(groups[-1:])
    own_s.wait()
    arrived(first.at[pl.ds(0, SLICES - 1)], e_sem.at[0])
    carried = jnp.concatenate([first[j] for j in range(SLICES)], axis=1)
    arrived(gbuf.at[:, 0], gc_sem.at[0])

    query = qt[cut(mine, qt.shape[0] // SLICES), :].astype(F32)
    whitened = omega * query
    half_x, half_w = NX // 2, width // 2
    for sweep in range(ITERS):
        if sweep:
            half = whitened.astype(BF16)
            for k in (0, 1):
                grads = gbuf[k * half_x : (k + 1) * half_x].reshape(half_x * CORES * n_z * rows, width)
                send_s[k] = dot_t(half, grads).astype(BF16)
                for i, to in enumerate(z_partners):
                    push(send_s.at[k], recv_s.at[k, i], s_sem.at[k], to)
            carried = []
            for k in (0, 1):
                if z_partners:
                    arrived(recv_s.at[k], s_sem.at[k])
                total = send_s[k].astype(F32)
                for i in range(len(z_partners)):
                    total = total + recv_s[k, i].astype(F32)
                carried.append(total.astype(BF16))
                if k == 0:
                    grads = gbuf[:half_x].reshape(half_x * CORES * n_z * rows, width)
                    part = jnp.dot(carried[0], grads, preferred_element_type=F32)
            grads = gbuf[half_x:].reshape(half_x * CORES * n_z * rows, width)
            part = part + jnp.dot(carried[1], grads, preferred_element_type=F32)
        else:
            grads = gbuf[...].reshape(SLICES * n_z * rows, width)
            part = jnp.dot(carried, grads, preferred_element_type=F32)
        send_t[sweep] = part.astype(BF16)
        for i, to in enumerate(y_partners):
            push(send_t.at[sweep], recv_t.at[sweep, i], t_sem.at[sweep], to)
        if y_partners:
            arrived(recv_t.at[sweep], t_sem.at[sweep])
        total = send_t[sweep].astype(F32)
        for i in range(len(y_partners)):
            total = total + recv_t[sweep, i].astype(F32)
        applied = total * (1.0 / total_rows)
        if sweep == 0:
            applied = omega * applied
        whitened = whitened + omega * (query - applied - DAMP * whitened)

    half = whitened.astype(BF16)
    for i, d in enumerate(along_z + [0]):
        there = z_at(d)
        send_o[there] = dot_t(half, gbuf[:, :, there].reshape(SLICES * rows, width))
        if d:
            push(send_o.at[there], recv_o.at[i], o_sem.at[0], z_partners[i])
    if z_partners:
        arrived(recv_o, o_sem.at[0])
    total = send_o[z]
    for i in range(len(z_partners)):
        total = total + recv_o[i]
    last[mine] = total
    for _, to in slice_partners:
        push(last.at[mine], last.at[mine], w_sem.at[0], to)
    arrived(last.at[pl.ds(0, SLICES - 1)], w_sem.at[0])
    turned[...] = last[...].reshape(qt.shape[0], SLICES * rows).T
    o_ref[...] = turned[cut(mine, rows), :]

    depart()


def body(n_grp, n_dev, train_grads, query_grads):
    rows, width = train_grads.shape
    block, queries = query_grads.shape
    n_z = n_dev // 4
    ny = n_grp * 2 // NX
    total_rows = rows * n_grp * n_dev
    omega = step_size(width, total_rows)
    slice_q = queries // SLICES
    held = 4 * block
    others_z, others_y = max(n_z - 1, 1), max(ny - 1, 1)
    vmem = pl.BlockSpec(memory_space=pltpu.VMEM)
    anywhere = pl.BlockSpec(memory_space=pl.ANY)
    dma = pltpu.SemaphoreType.DMA
    return pl.pallas_call(
        functools.partial(kernel, n_grp, n_z, omega, total_rows),
        name="influence",
        out_shape=jax.ShapeDtypeStruct((rows, queries), F32),
        in_specs=[anywhere, anywhere],
        out_specs=vmem,
        scratch_shapes=[
            pltpu.VMEM((rows, width), BF16),
            pltpu.VMEM((block, queries), BF16),
            pltpu.VMEM((NX, CORES, n_z, rows, held), BF16),
            pltpu.VMEM((4, block, queries), BF16),
            pltpu.VMEM((queries, held), BF16),
            pltpu.VMEM((n_z, rows, queries), BF16),
            pltpu.VMEM((others_z, rows, queries), BF16),
            pltpu.VMEM((n_z, rows, queries), BF16),
            pltpu.VMEM((SLICES, slice_q, n_z * rows), BF16),
            pltpu.VMEM((SLICES, slice_q, n_z * rows), BF16),
            pltpu.VMEM((2, slice_q, SLICES // 2 * n_z * rows), BF16),
            pltpu.VMEM((2, others_z, slice_q, SLICES // 2 * n_z * rows), BF16),
            pltpu.VMEM((ITERS, slice_q, held), BF16),
            pltpu.VMEM((ITERS, others_y, slice_q, held), BF16),
            pltpu.VMEM((n_z, slice_q, SLICES * rows), F32),
            pltpu.VMEM((others_z, slice_q, SLICES * rows), F32),
            pltpu.VMEM((SLICES, slice_q, SLICES * rows), F32),
            pltpu.VMEM((SLICES * rows, queries), F32),
            dma((5,)), dma((1,)), dma((1,)), dma((n_z,)), dma((n_z,)), dma((1,)),
            dma((1,)), dma((1,)), dma((1,)), dma((2,)), dma((ITERS,)), dma((1,)), dma((1,)),
        ],
        compiler_params=pltpu.CompilerParams(
            collective_id=0, has_side_effects=True, vmem_limit_bytes=55168 * 1024
        ),
    )(train_grads, query_grads)


def solution(mesh):
    return jax.shard_map(
        functools.partial(body, mesh.shape["grp"], mesh.shape["dev"]),
        mesh=mesh,
        in_specs=(P(("grp", "dev"), None), P("dev", None)),
        out_specs=P(("grp", "dev"), None),
        check_vma=False,
    )
```

```python
import functools
import math

import jax
import jax.numpy as jnp
from jax import lax
from jax.experimental import pallas as pl
from jax.experimental.pallas import tpu as pltpu
from jax.sharding import PartitionSpec as P

ITERS = 2
DAMP = 1.0
NX = 4
CORES = 2
SLICES = NX * CORES
MESH = pl.DeviceIdType.MESH
F32 = jnp.float32
BF16 = jnp.bfloat16


def step_size(width, total_rows):
    bound = (1.0 + math.sqrt(width / total_rows)) ** 2
    return 1.0 / (1.0 + 1.5 * bound)


def ring(d, n):
    return min(d, n - d)


def farthest_first(n):
    return sorted(range(1, n), key=lambda d: (-ring(d, n), d))


def dot_t(a, b):
    return lax.dot_general(a, b, (((1,), (1,)), ((), ())), preferred_element_type=F32)


def wide(value):
    high = value.astype(BF16)
    return jnp.concatenate([high, (value - high.astype(F32)).astype(BF16)], axis=0)


def folded(value):
    half = value.shape[0] // 2
    return value[:half] + value[half:]


def kernel(
    n_grp, n_z, omega, total_rows,
    g_ref, q_ref, o_ref,
    gl, ql, gbuf, qb, qt, send_f, recv_f, column, sums, first, send_s, recv_s, send_t, recv_t, swap, spread, send_o, recv_o,
    local_sem, send_sem, q_sem, gz_sem, gx_sem, gc_sem, f_sem, c_sem, e_sem, s_sem, t_sem, o_sem, w_sem,
):
    rows = g_ref.shape[0]
    block = q_ref.shape[0]
    width = 4 * block
    ny = n_grp * 2 // NX
    grp = lax.axis_index("grp")
    dev = lax.axis_index("dev")
    z, x_lo, core = dev // 4, lax.rem(dev // 2, 2), lax.rem(dev, 2)
    y, x = grp // 2, lax.rem(grp, 2) * 2 + x_lo
    mine = x * CORES + core

    def device(x_at, y_at, z_at, c):
        return (y_at * 2 + x_at // 2, z_at * 4 + lax.rem(x_at, 2) * 2 + c)

    def z_at(d):
        return lax.rem(z + d, n_z)

    along_z = farthest_first(n_z)
    z_partners = [device(x, y, z_at(d), core) for d in along_z]
    x_partners = [[device(lax.rem(x + d, NX), y, z, c) for c in (core, 1 - core)] for d in farthest_first(NX)]
    slice_partners = []
    for d in farthest_first(NX):
        there = lax.rem(x + d, NX)
        for c in (core, 1 - core):
            slice_partners.append((there * CORES + c, device(there, y, z, c)))
    slice_partners.append((x * CORES + 1 - core, device(x, y, z, 1 - core)))
    y_partners = [device(x, lax.rem(y + d, ny), z, core) for d in farthest_first(ny)]
    sibling = device(x, y, z, 1 - core)
    leaving = []

    def push(src, dst, sem, to):
        copy = pltpu.make_async_remote_copy(
            src_ref=src, dst_ref=dst, send_sem=send_sem.at[0], recv_sem=sem, device_id=to, device_id_type=MESH
        )
        copy.start()
        leaving.append(math.prod(src.shape) * src.dtype.itemsize)

    def arrived(like, sem):
        pltpu.make_async_copy(like, like, sem).wait()

    def depart():
        left = sum(leaving)
        leaving.clear()
        for like in (gbuf.at[0], gbuf.at[0, 0, 0], sums.at[0]):
            size = math.prod(like.shape) * like.dtype.itemsize
            while left >= size:
                arrived(like, send_sem.at[0])
                left -= size
        assert left == 0

    def cut(p, n):
        return pl.ds(pl.multiple_of(p * n, n), n)

    load_g = pltpu.make_async_copy(g_ref, gl, local_sem.at[0])
    load_q = pltpu.make_async_copy(q_ref, ql, local_sem.at[1])
    load_g.start()
    load_q.start()

    barrier = pltpu.get_barrier_semaphore()
    partners = z_partners + [to for pair in x_partners for to in pair] + y_partners + [sibling]
    for to in partners:
        pl.semaphore_signal(barrier, inc=1, device_id=to, device_id_type=MESH)
    pl.semaphore_wait(barrier, len(partners))

    load_g.wait()
    own_g = pltpu.make_async_copy(gl.at[:, cut(z, width)], gbuf.at[x, core, z], local_sem.at[2])
    own_g.start()
    for d, to in zip(along_z, z_partners):
        push(gl.at[:, cut(z_at(d), width)], gbuf.at[x, core, z], gz_sem.at[n_z - d], to)

    load_q.wait()
    spot = qb.at[x_lo * 2 + core]
    own_q = pltpu.make_async_copy(ql, spot, local_sem.at[3])
    own_q.start()
    near = device(x + 1 - 2 * x_lo, y, z, core), device(x + 1 - 2 * x_lo, y, z, 1 - core)
    for to in (sibling, *near):
        push(ql, spot, q_sem.at[0], to)

    groups = [[0]] + [[d for d in along_z if ring(d, n_z) == far] for far in range(n_z // 2, 0, -1)]
    own_g.wait()
    for group in groups:
        for d in group:
            here = gbuf.at[x, core, z_at(d)]
            if d:
                arrived(here, gz_sem.at[d])
            for same, _ in x_partners:
                push(here, here, gx_sem.at[d], same)
        if group == [0]:
            own_q.wait()
            arrived(qb.at[pl.ds(0, 3)], q_sem.at[0])
        pieces = [gbuf[x, core, z_at(d)] for d in group]
        pieces = pieces[0] if len(pieces) == 1 else jnp.concatenate(pieces, axis=0)
        part = jnp.dot(pieces, qb[...].reshape(width, qb.shape[-1]), preferred_element_type=F32).astype(BF16)
        for i, d in enumerate(group):
            send_f[d] = part[i * rows : (i + 1) * rows]
            if d:
                push(send_f.at[d], recv_f.at[d - 1], f_sem.at[0], device(x, y, z_at(d), core))
    qt[...] = qb[...].reshape(width, qb.shape[-1]).astype(F32).T.astype(BF16)
    if z_partners:
        arrived(recv_f, f_sem.at[0])
    total = send_f[0].astype(F32)
    for i in range(len(z_partners)):
        total = total + recv_f[i].astype(F32)
    column[z] = total.astype(BF16)
    for to in z_partners:
        push(column.at[z], column.at[z], c_sem.at[0], to)

    def across(groups):
        for group in groups:
            for d in group:
                arrived(gbuf.at[pl.ds(0, NX - 1), 0, 0], gx_sem.at[d])
                here = gbuf.at[:, core, z_at(d)]
                push(here, here, gc_sem.at[0], sibling)

    across(groups[:-1])
    if z_partners:
        arrived(column.at[pl.ds(0, n_z - 1)], c_sem.at[0])
    total = column[...].reshape(n_z * rows, qb.shape[-1]).astype(F32).T
    sums[...] = total.astype(BF16).reshape(sums.shape)
    own_s = pltpu.make_async_copy(sums.at[mine], first.at[mine], local_sem.at[4])
    own_s.start()
    for there, to in slice_partners:
        push(sums.at[there], first.at[mine], e_sem.at[0], to)
    across(groups[-1:])
    own_s.wait()
    arrived(first.at[pl.ds(0, SLICES - 1)], e_sem.at[0])
    carried = jnp.concatenate([first[j] for j in range(SLICES)], axis=1)
    arrived(gbuf.at[:, 0], gc_sem.at[0])

    query = qt[cut(mine, qt.shape[0] // SLICES), :].astype(F32)
    whitened = omega * query
    half_x, slice_q = NX // 2, qt.shape[0] // SLICES
    for sweep in range(ITERS):
        if sweep:
            both = wide(whitened)
            own = []
            for k in (0, 1):
                grads = gbuf[k * half_x : (k + 1) * half_x].reshape(half_x * CORES * n_z * rows, width)
                own.append(folded(dot_t(both, grads)))
                send_s[k] = own[k].astype(BF16)
                for i, to in enumerate(z_partners):
                    push(send_s.at[k], recv_s.at[k, i], s_sem.at[k], to)
            part = jnp.zeros((slice_q, width), F32)
            for k in (0, 1):
                if z_partners:
                    arrived(recv_s.at[k], s_sem.at[k])
                total = own[k]
                for i in range(len(z_partners)):
                    total = total + recv_s[k, i].astype(F32)
                grads = gbuf[k * half_x : (k + 1) * half_x].reshape(half_x * CORES * n_z * rows, width)
                part = part + folded(jnp.dot(wide(total), grads, preferred_element_type=F32))
        else:
            grads = gbuf[...].reshape(SLICES * n_z * rows, width)
            part = jnp.dot(carried, grads, preferred_element_type=F32)
        send_t[sweep] = part.astype(BF16)
        for i, to in enumerate(y_partners):
            push(send_t.at[sweep], recv_t.at[sweep, i], t_sem.at[sweep], to)
        if y_partners:
            arrived(recv_t.at[sweep], t_sem.at[sweep])
        total = part
        for i in range(len(y_partners)):
            total = total + recv_t[sweep, i].astype(F32)
        applied = total * (1.0 / total_rows)
        if sweep == 0:
            applied = omega * applied
        whitened = whitened + omega * (query - applied - DAMP * whitened)

    swap[core] = whitened.astype(BF16)
    push(swap.at[core], swap.at[core], w_sem.at[0], sibling)
    spread[...] = jnp.zeros_like(spread)
    arrived(swap.at[0], w_sem.at[0])
    at = lax.rem(x, 2) * CORES
    for c in range(CORES):
        spread[cut(at + c, slice_q), :] = swap[c]
    over_x = farthest_first(NX) + [0]
    over_z = along_z + [0]
    rows_h = rows // 2
    for k, dx in enumerate(over_x):
        there = lax.rem(x + dx, NX)
        part = dot_t(gbuf[there, core].reshape(n_z * rows, width), spread[...]).reshape(n_z, rows, 128)
        send_o[there] = part[:, :rows_h] + pltpu.roll(part[:, rows_h:], 64, 2)
        for i, dz in enumerate(over_z):
            if dx or dz:
                to = device(there, y, z_at(dz), core)
                push(send_o.at[there, z_at(dz)], recv_o.at[k * n_z + i], o_sem.at[0], to)
    depart()
    arrived(recv_o.at[pl.ds(0, NX * n_z - 1)], o_sem.at[0])
    lower = jnp.zeros((rows_h, 128), F32)
    upper = jnp.zeros((rows_h, 128), F32)
    for k, dx in enumerate(over_x):
        total = send_o[x, z] if dx == 0 else recv_o[k * n_z + n_z - 1]
        for i in range(n_z - 1):
            total = total + recv_o[k * n_z + i]
        source = lax.rem(x + NX - dx, NX)
        lower = lower + jnp.where(source < 2, total, 0.0)
        upper = upper + jnp.where(source < 2, 0.0, total)
    left = lax.broadcasted_iota(jnp.int32, lower.shape, 1) < 64
    o_ref[0:rows_h, :] = jnp.where(left, lower, pltpu.roll(upper, 64, 1))
    o_ref[rows_h:rows, :] = jnp.where(left, pltpu.roll(lower, 64, 1), upper)


def body(n_grp, n_dev, train_grads, query_grads):
    rows, width = train_grads.shape
    block, queries = query_grads.shape
    n_z = n_dev // 4
    ny = n_grp * 2 // NX
    total_rows = rows * n_grp * n_dev
    omega = step_size(width, total_rows)
    slice_q = queries // SLICES
    held = 4 * block
    others_z, others_y = max(n_z - 1, 1), max(ny - 1, 1)
    vmem = pl.BlockSpec(memory_space=pltpu.VMEM)
    anywhere = pl.BlockSpec(memory_space=pl.ANY)
    dma = pltpu.SemaphoreType.DMA
    return pl.pallas_call(
        functools.partial(kernel, n_grp, n_z, omega, total_rows),
        name="influence",
        out_shape=jax.ShapeDtypeStruct((rows, queries), F32),
        in_specs=[anywhere, anywhere],
        out_specs=vmem,
        scratch_shapes=[
            pltpu.VMEM((rows, width), BF16),
            pltpu.VMEM((block, queries), BF16),
            pltpu.VMEM((NX, CORES, n_z, rows, held), BF16),
            pltpu.VMEM((4, block, queries), BF16),
            pltpu.VMEM((queries, held), BF16),
            pltpu.VMEM((n_z, rows, queries), BF16),
            pltpu.VMEM((others_z, rows, queries), BF16),
            pltpu.VMEM((n_z, rows, queries), BF16),
            pltpu.VMEM((SLICES, slice_q, n_z * rows), BF16),
            pltpu.VMEM((SLICES, slice_q, n_z * rows), BF16),
            pltpu.VMEM((2, slice_q, SLICES // 2 * n_z * rows), BF16),
            pltpu.VMEM((2, others_z, slice_q, SLICES // 2 * n_z * rows), BF16),
            pltpu.VMEM((ITERS, slice_q, held), BF16),
            pltpu.VMEM((ITERS, others_y, slice_q, held), BF16),
            pltpu.VMEM((CORES, slice_q, held), BF16),
            pltpu.VMEM((queries, held), BF16),
            pltpu.VMEM((NX, n_z, rows // 2, queries), F32),
            pltpu.VMEM((NX * n_z, rows // 2, queries), F32),
            dma((5,)), dma((1,)), dma((1,)), dma((n_z,)), dma((n_z,)), dma((1,)),
            dma((1,)), dma((1,)), dma((1,)), dma((2,)), dma((ITERS,)), dma((1,)), dma((1,)),
        ],
        compiler_params=pltpu.CompilerParams(
            collective_id=0, has_side_effects=True, vmem_limit_bytes=55168 * 1024
        ),
    )(train_grads, query_grads)


def solution(mesh):
    return jax.shard_map(
        functools.partial(body, mesh.shape["grp"], mesh.shape["dev"]),
        mesh=mesh,
        in_specs=(P(("grp", "dev"), None), P("dev", None)),
        out_specs=P(("grp", "dev"), None),
        check_vma=False,
    )
```

```python
import functools
import math

import jax
import jax.numpy as jnp
from jax import lax
from jax.experimental import pallas as pl
from jax.experimental.pallas import tpu as pltpu
from jax.sharding import PartitionSpec as P

ITERS = 2
DAMP = 1.0
NX = 4
CORES = 2
SLICES = NX * CORES
MESH = pl.DeviceIdType.MESH
F32 = jnp.float32
BF16 = jnp.bfloat16


def step_size(width, total_rows):
    bound = (1.0 + math.sqrt(width / total_rows)) ** 2
    return 1.0 / (1.0 + 1.5 * bound)


def ring(d, n):
    return min(d, n - d)


def farthest_first(n):
    return sorted(range(1, n), key=lambda d: (-ring(d, n), d))


def dot_t(a, b):
    return lax.dot_general(a, b, (((1,), (1,)), ((), ())), preferred_element_type=F32)


def wide(value):
    high = value.astype(BF16)
    return jnp.concatenate([high, (value - high.astype(F32)).astype(BF16)], axis=0)


def folded(value):
    half = value.shape[0] // 2
    return value[:half] + value[half:]


def kernel(
    n_grp, n_z, omega, total_rows,
    g_ref, q_ref, o_ref,
    gl, ql, gbuf, qb, qt, send_f, recv_f, column, sums, recv_e, first, send_s, recv_s, send_t, recv_t, cross_t, swap, spread, send_o, recv_o,
    local_sem, send_sem, q_sem, gz_sem, gx_sem, gc_sem, f_sem, ready_sem, e_sem, s_sem, t_sem, o_sem, w_sem,
):
    rows = g_ref.shape[0]
    block = q_ref.shape[0]
    width = 4 * block
    ny = n_grp * 2 // NX
    grp = lax.axis_index("grp")
    dev = lax.axis_index("dev")
    z, x_lo, core = dev // 4, lax.rem(dev // 2, 2), lax.rem(dev, 2)
    y, x = grp // 2, lax.rem(grp, 2) * 2 + x_lo
    mine = x * CORES + core

    def device(x_at, y_at, z_at, c):
        return (y_at * 2 + x_at // 2, z_at * 4 + lax.rem(x_at, 2) * 2 + c)

    def z_at(d):
        return lax.rem(z + d, n_z)

    along_z = farthest_first(n_z)
    z_partners = [device(x, y, z_at(d), core) for d in along_z]
    z_crossed = [device(x, y, z_at(d), 1 - core) for d in along_z]
    x_partners = [[device(lax.rem(x + d, NX), y, z, c) for c in (core, 1 - core)] for d in farthest_first(NX)]
    y_partners = [device(x, lax.rem(y + d, ny), z, core) for d in farthest_first(ny)]
    sibling = device(x, y, z, 1 - core)
    y_crossed = [device(x, lax.rem(y + d, ny), z, 1 - core) for d in farthest_first(ny)]
    leaving = []

    def push(src, dst, sem, to):
        copy = pltpu.make_async_remote_copy(
            src_ref=src, dst_ref=dst, send_sem=send_sem.at[0], recv_sem=sem, device_id=to, device_id_type=MESH
        )
        copy.start()
        leaving.append(math.prod(src.shape) * src.dtype.itemsize)

    def arrived(like, sem):
        pltpu.make_async_copy(like, like, sem).wait()

    def depart():
        left = sum(leaving)
        leaving.clear()
        for like in (gbuf.at[0], gbuf.at[0, 0, 0], sums.at[0]):
            size = math.prod(like.shape) * like.dtype.itemsize
            while left >= size:
                arrived(like, send_sem.at[0])
                left -= size
        assert left == 0

    def cut(p, n):
        return pl.ds(pl.multiple_of(p * n, n), n)

    load_g = pltpu.make_async_copy(g_ref, gl, local_sem.at[0])
    load_q = pltpu.make_async_copy(q_ref, ql, local_sem.at[1])
    load_g.start()
    load_q.start()

    barrier = pltpu.get_barrier_semaphore()
    partners = z_partners + z_crossed + [to for pair in x_partners for to in pair] + y_partners + [sibling]
    for to in partners:
        pl.semaphore_signal(barrier, inc=1, device_id=to, device_id_type=MESH)
    pl.semaphore_wait(barrier, len(partners))

    load_g.wait()
    own_g = pltpu.make_async_copy(gl.at[:, cut(z, width)], gbuf.at[x, core, z], local_sem.at[2])
    own_g.start()
    groups = [[0]] + [[d for d in along_z if ring(d, n_z) == far] for far in range(n_z // 2, 0, -1)]
    if len(groups) > 2:
        groups.insert(1, groups.pop())
    for group in groups[1:]:
        for d in group:
            push(gl.at[:, cut(z_at(d), width)], gbuf.at[x, core, z], gz_sem.at[n_z - d], device(x, y, z_at(d), core))

    load_q.wait()
    spot = qb.at[x_lo * 2 + core]
    own_q = pltpu.make_async_copy(ql, spot, local_sem.at[3])
    own_q.start()
    near = device(x + 1 - 2 * x_lo, y, z, core), device(x + 1 - 2 * x_lo, y, z, 1 - core)
    for to in (sibling, *near):
        push(ql, spot, q_sem.at[0], to)

    def across(groups):
        for group in groups:
            for d in group:
                arrived(gbuf.at[pl.ds(0, NX - 1), 0, 0], gx_sem.at[d])
                here = gbuf.at[:, core, z_at(d)]
                push(here, here, gc_sem.at[0], sibling)

    own_g.wait()
    for group in groups:
        for d in group:
            here = gbuf.at[x, core, z_at(d)]
            if d:
                arrived(here, gz_sem.at[d])
            for same, _ in x_partners:
                push(here, here, gx_sem.at[d], same)
        if group == [0]:
            own_q.wait()
            arrived(qb.at[pl.ds(0, 3)], q_sem.at[0])
        pieces = [gbuf[x, core, z_at(d)] for d in group]
        pieces = pieces[0] if len(pieces) == 1 else jnp.concatenate(pieces, axis=0)
        part = jnp.dot(pieces, qb[...].reshape(width, qb.shape[-1]), preferred_element_type=F32).astype(BF16)
        for i, d in enumerate(group):
            send_f[d] = part[i * rows : (i + 1) * rows]
            if d:
                push(send_f.at[d], recv_f.at[0, d], f_sem.at[0], device(x, y, z_at(d), core))
                push(send_f.at[d], recv_f.at[1, d], f_sem.at[1], device(x, y, z_at(d), 1 - core))
            else:
                push(send_f.at[d], recv_f.at[1, d], f_sem.at[1], sibling)

    over_x = farthest_first(NX) + [0]
    over_z = along_z + [0]
    for same, _ in x_partners:
        pl.semaphore_signal(ready_sem, inc=1, device_id=same, device_id_type=MESH)
    qt[...] = qb[...].reshape(width, qb.shape[-1]).astype(F32).T.astype(BF16)
    column[...] = jnp.zeros_like(column)
    spread[...] = jnp.zeros_like(spread)
    across(groups[:3])
    arrived(recv_f.at[1], f_sem.at[1])
    if z_partners:
        arrived(recv_f.at[0, pl.ds(0, n_z - 1)], f_sem.at[0])
    total = send_f[0].astype(F32)
    for d in range(1, n_z):
        total = total + recv_f[0, d].astype(F32)
    column[cut(mine, rows), :] = total
    total = recv_f[1, 0].astype(F32)
    for d in range(1, n_z):
        total = total + recv_f[1, d].astype(F32)
    column[cut(x * CORES + 1 - core, rows), :] = total
    sums[...] = column[...].T.astype(BF16).reshape(sums.shape)
    pl.semaphore_wait(ready_sem, NX - 1)
    for k, dx in enumerate(over_x):
        there = lax.rem(x + dx, NX)
        for i, dz in enumerate(over_z):
            if dx or dz:
                to = device(there, y, z_at(dz), core)
                push(sums.at[there * CORES + core], recv_e.at[k * n_z + i], e_sem.at[0], to)
    across(groups[3:])
    arrived(recv_e.at[pl.ds(0, NX * n_z - 1)], e_sem.at[0])
    for i, dz in enumerate(over_z):
        total = sums[mine] if dz == 0 else recv_e[(NX - 1) * n_z + i]
        for k in range(NX - 1):
            total = total + recv_e[k * n_z + i]
        first[z_at(n_z - dz)] = total
    carried = jnp.concatenate([first[there] for there in range(n_z)], axis=1)
    arrived(gbuf.at[:, 0], gc_sem.at[0])

    query = qt[cut(mine, qt.shape[0] // SLICES), :].astype(F32)
    whitened = omega * query
    half_x, slice_q = NX // 2, qt.shape[0] // SLICES
    for sweep in range(ITERS):
        if sweep:
            both = wide(whitened)
            own = []
            for k in (0, 1):
                grads = gbuf[k * half_x : (k + 1) * half_x].reshape(half_x * CORES * n_z * rows, width)
                own.append(folded(dot_t(both, grads)))
                send_s[k] = own[k].astype(BF16)
                for i, to in enumerate(z_partners):
                    push(send_s.at[k], recv_s.at[k, i], s_sem.at[k], to)
            part = jnp.zeros((slice_q, width), F32)
            for k in (0, 1):
                if z_partners:
                    arrived(recv_s.at[k], s_sem.at[k])
                total = own[k]
                for i in range(len(z_partners)):
                    total = total + recv_s[k, i].astype(F32)
                grads = gbuf[k * half_x : (k + 1) * half_x].reshape(half_x * CORES * n_z * rows, width)
                part = part + folded(jnp.dot(wide(total), grads, preferred_element_type=F32))
        else:
            grads = [gbuf[:, :, there].reshape(SLICES * rows, width) for there in range(n_z)]
            part = jnp.dot(carried, jnp.concatenate(grads, axis=0), preferred_element_type=F32)
        send_t[sweep] = part.astype(BF16)
        if sweep == ITERS - 1:
            for i, to in enumerate(y_crossed + [sibling]):
                push(send_t.at[sweep], cross_t.at[i], w_sem.at[1], to)
        for i, to in enumerate(y_partners):
            push(send_t.at[sweep], recv_t.at[sweep, i], t_sem.at[sweep], to)
        if y_partners:
            arrived(recv_t.at[sweep], t_sem.at[sweep])
        total = part
        for i in range(len(y_partners)):
            total = total + recv_t[sweep, i].astype(F32)
        applied = total * (1.0 / total_rows)
        if sweep == 0:
            applied = omega * applied
        whitened = whitened + omega * (query - applied - DAMP * whitened)
        if sweep == ITERS - 2:
            swap[core] = whitened
            push(swap.at[core], swap.at[core], w_sem.at[0], sibling)

    other = x * CORES + 1 - core
    arrived(swap.at[0], w_sem.at[0])
    arrived(cross_t, w_sem.at[1])
    total = cross_t[0].astype(F32)
    for i in range(1, ny):
        total = total + cross_t[i].astype(F32)
    crossed = swap[1 - core]
    query = qt[cut(other, slice_q), :].astype(F32)
    crossed = crossed + omega * (query - total * (1.0 / total_rows) - DAMP * crossed)

    at = lax.rem(x, 2) * CORES
    spread[cut(at + core, slice_q), :] = whitened.astype(BF16)
    spread[cut(at + 1 - core, slice_q), :] = crossed.astype(BF16)
    rows_h = rows // 2
    for k, dx in enumerate(over_x):
        there = lax.rem(x + dx, NX)
        part = dot_t(gbuf[there, core].reshape(n_z * rows, width), spread[...]).reshape(n_z, rows, 128)
        send_o[there] = part[:, :rows_h] + pltpu.roll(part[:, rows_h:], 64, 2)
        for i, dz in enumerate(over_z):
            if dx or dz:
                to = device(there, y, z_at(dz), core)
                push(send_o.at[there, z_at(dz)], recv_o.at[k * n_z + i], o_sem.at[0], to)
    depart()
    arrived(recv_o.at[pl.ds(0, NX * n_z - 1)], o_sem.at[0])
    lower = jnp.zeros((rows_h, 128), F32)
    upper = jnp.zeros((rows_h, 128), F32)
    for k, dx in enumerate(over_x):
        total = send_o[x, z] if dx == 0 else recv_o[k * n_z + n_z - 1]
        for i in range(n_z - 1):
            total = total + recv_o[k * n_z + i]
        source = lax.rem(x + NX - dx, NX)
        lower = lower + jnp.where(source < 2, total, 0.0)
        upper = upper + jnp.where(source < 2, 0.0, total)
    left = lax.broadcasted_iota(jnp.int32, lower.shape, 1) < 64
    o_ref[0:rows_h, :] = jnp.where(left, lower, pltpu.roll(upper, 64, 1))
    o_ref[rows_h:rows, :] = jnp.where(left, pltpu.roll(lower, 64, 1), upper)


def body(n_grp, n_dev, train_grads, query_grads):
    rows, width = train_grads.shape
    block, queries = query_grads.shape
    n_z = n_dev // 4
    ny = n_grp * 2 // NX
    total_rows = rows * n_grp * n_dev
    omega = step_size(width, total_rows)
    slice_q = queries // SLICES
    held = 4 * block
    others_z, others_y = max(n_z - 1, 1), max(ny - 1, 1)
    vmem = pl.BlockSpec(memory_space=pltpu.VMEM)
    anywhere = pl.BlockSpec(memory_space=pl.ANY)
    dma = pltpu.SemaphoreType.DMA
    return pl.pallas_call(
        functools.partial(kernel, n_grp, n_z, omega, total_rows),
        name="influence",
        out_shape=jax.ShapeDtypeStruct((rows, queries), F32),
        in_specs=[anywhere, anywhere],
        out_specs=vmem,
        scratch_shapes=[
            pltpu.VMEM((rows, width), BF16),
            pltpu.VMEM((block, queries), BF16),
            pltpu.VMEM((NX, CORES, n_z, rows, held), BF16),
            pltpu.VMEM((4, block, queries), BF16),
            pltpu.VMEM((queries, held), BF16),
            pltpu.VMEM((n_z, rows, queries), BF16),
            pltpu.VMEM((CORES, n_z, rows, queries), BF16),
            pltpu.VMEM((SLICES * rows, queries), F32),
            pltpu.VMEM((SLICES, slice_q, SLICES * rows), BF16),
            pltpu.VMEM((NX * n_z, slice_q, SLICES * rows), BF16),
            pltpu.VMEM((n_z, slice_q, SLICES * rows), BF16),
            pltpu.VMEM((2, slice_q, SLICES // 2 * n_z * rows), BF16),
            pltpu.VMEM((2, others_z, slice_q, SLICES // 2 * n_z * rows), BF16),
            pltpu.VMEM((ITERS, slice_q, held), BF16),
            pltpu.VMEM((ITERS, others_y, slice_q, held), BF16),
            pltpu.VMEM((ny, slice_q, held), BF16),
            pltpu.VMEM((CORES, slice_q, held), F32),
            pltpu.VMEM((queries, held), BF16),
            pltpu.VMEM((NX, n_z, rows // 2, queries), F32),
            pltpu.VMEM((NX * n_z, rows // 2, queries), F32),
            dma((5,)), dma((1,)), dma((1,)), dma((n_z,)), dma((n_z,)), dma((1,)),
            dma((2,)), pltpu.SemaphoreType.REGULAR, dma((1,)), dma((2,)), dma((ITERS,)), dma((1,)), dma((2,)),
        ],
        compiler_params=pltpu.CompilerParams(
            collective_id=0, has_side_effects=True, vmem_limit_bytes=55168 * 1024
        ),
    )(train_grads, query_grads)


def solution(mesh):
    return jax.shard_map(
        functools.partial(body, mesh.shape["grp"], mesh.shape["dev"]),
        mesh=mesh,
        in_specs=(P(("grp", "dev"), None), P("dev", None)),
        out_specs=P(("grp", "dev"), None),
        check_vma=False,
    )
```

```python
import functools
import math

import jax
import jax.numpy as jnp
from jax import lax
from jax.experimental import pallas as pl
from jax.experimental.pallas import tpu as pltpu
from jax.sharding import PartitionSpec as P

ITERS = 2
DAMP = 1.0
NX = 4
CORES = 2
SLICES = NX * CORES
MESH = pl.DeviceIdType.MESH
F32 = jnp.float32
BF16 = jnp.bfloat16


def step_size(width, total_rows):
    bound = (1.0 + math.sqrt(width / total_rows)) ** 2
    return 1.0 / (1.0 + 1.5 * bound)


def ring(d, n):
    return min(d, n - d)


def farthest_first(n):
    return sorted(range(1, n), key=lambda d: (-ring(d, n), d))


def dot_t(a, b):
    return lax.dot_general(a, b, (((1,), (1,)), ((), ())), preferred_element_type=F32)


def wide(value):
    high = value.astype(BF16)
    return jnp.concatenate([high, (value - high.astype(F32)).astype(BF16)], axis=0)


def folded(value):
    half = value.shape[0] // 2
    return value[:half] + value[half:]


def kernel(
    n_grp, n_z, omega, total_rows,
    g_ref, q_ref, o_ref,
    gl, ql, gbuf, qb, qt, send_f, recv_f, column, sums, recv_e, first, send_s, recv_s, send_t, recv_t, cross_t, swap, spread, send_o, recv_o,
    local_sem, send_sem, q_sem, gz_sem, gx_sem, gc_sem, f_sem, ready_sem, e_sem, s_sem, t_sem, o_sem, w_sem,
):
    rows = g_ref.shape[0]
    block = q_ref.shape[0]
    width = 4 * block
    ny = n_grp * 2 // NX
    grp = lax.axis_index("grp")
    dev = lax.axis_index("dev")
    z, x_lo, core = dev // 4, lax.rem(dev // 2, 2), lax.rem(dev, 2)
    y, x = grp // 2, lax.rem(grp, 2) * 2 + x_lo
    mine = x * CORES + core

    def device(x_at, y_at, z_at, c):
        return (y_at * 2 + x_at // 2, z_at * 4 + lax.rem(x_at, 2) * 2 + c)

    def z_at(d):
        return lax.rem(z + d, n_z)

    along_z = farthest_first(n_z)
    z_partners = [device(x, y, z_at(d), core) for d in along_z]
    z_crossed = [device(x, y, z_at(d), 1 - core) for d in along_z]
    x_partners = [[device(lax.rem(x + d, NX), y, z, c) for c in (core, 1 - core)] for d in farthest_first(NX)]
    y_partners = [device(x, lax.rem(y + d, ny), z, core) for d in farthest_first(ny)]
    sibling = device(x, y, z, 1 - core)
    y_crossed = [device(x, lax.rem(y + d, ny), z, 1 - core) for d in farthest_first(ny)]
    leaving = []

    def push(src, dst, sem, to):
        copy = pltpu.make_async_remote_copy(
            src_ref=src, dst_ref=dst, send_sem=send_sem.at[0], recv_sem=sem, device_id=to, device_id_type=MESH
        )
        copy.start()
        leaving.append(math.prod(src.shape) * src.dtype.itemsize)

    def arrived(like, sem):
        pltpu.make_async_copy(like, like, sem).wait()

    def depart():
        left = sum(leaving)
        leaving.clear()
        for like in (gbuf.at[0], gbuf.at[0, 0, 0], sums.at[0]):
            size = math.prod(like.shape) * like.dtype.itemsize
            while left >= size:
                arrived(like, send_sem.at[0])
                left -= size
        assert left == 0

    def cut(p, n):
        return pl.ds(pl.multiple_of(p * n, n), n)

    load_g = pltpu.make_async_copy(g_ref, gl, local_sem.at[0])
    load_q = pltpu.make_async_copy(q_ref, ql, local_sem.at[1])
    load_g.start()
    load_q.start()

    barrier = pltpu.get_barrier_semaphore()
    partners = z_partners + z_crossed + [to for pair in x_partners for to in pair] + y_partners + [sibling]
    for to in partners:
        pl.semaphore_signal(barrier, inc=1, device_id=to, device_id_type=MESH)
    pl.semaphore_wait(barrier, len(partners))

    load_g.wait()
    own_g = pltpu.make_async_copy(gl.at[:, cut(z, width)], gbuf.at[x, core, z], local_sem.at[2])
    own_g.start()
    groups = [[0]] + [[d for d in along_z if ring(d, n_z) == far] for far in range(n_z // 2, 0, -1)]
    if len(groups) > 1:
        groups[0] = groups[0] + groups.pop()
    for group in groups:
        for d in group:
            if d:
                push(gl.at[:, cut(z_at(d), width)], gbuf.at[x, core, z], gz_sem.at[n_z - d], device(x, y, z_at(d), core))

    load_q.wait()
    spot = qb.at[x_lo * 2 + core]
    own_q = pltpu.make_async_copy(ql, spot, local_sem.at[3])
    own_q.start()
    near = device(x + 1 - 2 * x_lo, y, z, core), device(x + 1 - 2 * x_lo, y, z, 1 - core)
    for to in (sibling, *near):
        push(ql, spot, q_sem.at[0], to)

    def across(groups):
        for group in groups:
            for d in group:
                arrived(gbuf.at[pl.ds(0, NX - 1), 0, 0], gx_sem.at[d])
                here = gbuf.at[:, core, z_at(d)]
                push(here, here, gc_sem.at[0], sibling)

    own_g.wait()
    for group in groups:
        for d in group:
            here = gbuf.at[x, core, z_at(d)]
            if d:
                arrived(here, gz_sem.at[d])
            for same, _ in x_partners:
                push(here, here, gx_sem.at[d], same)
        if 0 in group:
            own_q.wait()
            arrived(qb.at[pl.ds(0, 3)], q_sem.at[0])
        pieces = [gbuf[x, core, z_at(d)] for d in group]
        pieces = pieces[0] if len(pieces) == 1 else jnp.concatenate(pieces, axis=0)
        part = jnp.dot(pieces, qb[...].reshape(width, qb.shape[-1]), preferred_element_type=F32).astype(BF16)
        for i, d in enumerate(group):
            send_f[d] = part[i * rows : (i + 1) * rows]
            if d:
                push(send_f.at[d], recv_f.at[0, d], f_sem.at[0], device(x, y, z_at(d), core))
                push(send_f.at[d], recv_f.at[1, d], f_sem.at[1], device(x, y, z_at(d), 1 - core))
            else:
                push(send_f.at[d], recv_f.at[1, d], f_sem.at[1], sibling)

    over_x = farthest_first(NX) + [0]
    over_z = along_z + [0]
    far = {(k, i): ring(dx, NX) + ring(dz, n_z) for k, dx in enumerate(over_x) for i, dz in enumerate(over_z)}
    by_distance = sorted((pair for pair in far if far[pair]), key=lambda pair: -far[pair])
    for same, _ in x_partners:
        pl.semaphore_signal(ready_sem, inc=1, device_id=same, device_id_type=MESH)
    qt[...] = qb[...].reshape(width, qb.shape[-1]).astype(F32).T.astype(BF16)
    column[...] = jnp.zeros_like(column)
    spread[...] = jnp.zeros_like(spread)
    across(groups[:2])
    arrived(recv_f.at[1], f_sem.at[1])
    if z_partners:
        arrived(recv_f.at[0, pl.ds(0, n_z - 1)], f_sem.at[0])
    total = send_f[0].astype(F32)
    for d in range(1, n_z):
        total = total + recv_f[0, d].astype(F32)
    column[cut(mine, rows), :] = total
    total = recv_f[1, 0].astype(F32)
    for d in range(1, n_z):
        total = total + recv_f[1, d].astype(F32)
    column[cut(x * CORES + 1 - core, rows), :] = total
    sums[...] = column[...].T.astype(BF16).reshape(sums.shape)
    pl.semaphore_wait(ready_sem, NX - 1)
    for k, i in by_distance:
        there = lax.rem(x + over_x[k], NX)
        to = device(there, y, z_at(over_z[i]), core)
        push(sums.at[there * CORES + core], recv_e.at[k * n_z + i], e_sem.at[0], to)
    across(groups[2:])
    arrived(recv_e.at[pl.ds(0, NX * n_z - 1)], e_sem.at[0])
    for i, dz in enumerate(over_z):
        total = sums[mine] if dz == 0 else recv_e[(NX - 1) * n_z + i]
        for k in range(NX - 1):
            total = total + recv_e[k * n_z + i]
        first[z_at(n_z - dz)] = total
    carried = jnp.concatenate([first[there] for there in range(n_z)], axis=1)
    arrived(gbuf.at[:, 0], gc_sem.at[0])

    query = qt[cut(mine, qt.shape[0] // SLICES), :].astype(F32)
    whitened = omega * query
    half_x, slice_q = NX // 2, qt.shape[0] // SLICES
    for sweep in range(ITERS):
        if sweep:
            both = wide(whitened)
            own = []
            for k in (0, 1):
                grads = gbuf[k * half_x : (k + 1) * half_x].reshape(half_x * CORES * n_z * rows, width)
                own.append(folded(dot_t(both, grads)))
                send_s[k] = own[k].astype(BF16)
                for i, to in enumerate(z_partners):
                    push(send_s.at[k], recv_s.at[k, i], s_sem.at[k], to)
            part = jnp.zeros((slice_q, width), F32)
            for k in (0, 1):
                if z_partners:
                    arrived(recv_s.at[k], s_sem.at[k])
                total = own[k]
                for i in range(len(z_partners)):
                    total = total + recv_s[k, i].astype(F32)
                grads = gbuf[k * half_x : (k + 1) * half_x].reshape(half_x * CORES * n_z * rows, width)
                part = part + folded(jnp.dot(wide(total), grads, preferred_element_type=F32))
        else:
            grads = [gbuf[:, :, there].reshape(SLICES * rows, width) for there in range(n_z)]
            part = jnp.dot(carried, jnp.concatenate(grads, axis=0), preferred_element_type=F32)
        send_t[sweep] = part.astype(BF16)
        if sweep == ITERS - 1:
            for i, to in enumerate(y_crossed + [sibling]):
                push(send_t.at[sweep], cross_t.at[i], w_sem.at[1], to)
        for i, to in enumerate(y_partners):
            push(send_t.at[sweep], recv_t.at[sweep, i], t_sem.at[sweep], to)
        if y_partners:
            arrived(recv_t.at[sweep], t_sem.at[sweep])
        total = part
        for i in range(len(y_partners)):
            total = total + recv_t[sweep, i].astype(F32)
        applied = total * (1.0 / total_rows)
        if sweep == 0:
            applied = omega * applied
        whitened = whitened + omega * (query - applied - DAMP * whitened)
        if sweep == ITERS - 2:
            swap[core] = whitened
            push(swap.at[core], swap.at[core], w_sem.at[0], sibling)

    other = x * CORES + 1 - core
    arrived(swap.at[0], w_sem.at[0])
    arrived(cross_t, w_sem.at[1])
    total = cross_t[0].astype(F32)
    for i in range(1, ny):
        total = total + cross_t[i].astype(F32)
    crossed = swap[1 - core]
    query = qt[cut(other, slice_q), :].astype(F32)
    crossed = crossed + omega * (query - total * (1.0 / total_rows) - DAMP * crossed)

    at = lax.rem(x, 2) * CORES
    spread[cut(at + core, slice_q), :] = whitened.astype(BF16)
    spread[cut(at + 1 - core, slice_q), :] = crossed.astype(BF16)
    rows_h = rows // 2

    def put(pair):
        k, i = pair
        there, z_there = lax.rem(x + over_x[k], NX), z_at(over_z[i])
        push(send_o.at[there, z_there], recv_o.at[k * n_z + i], o_sem.at[0], device(there, y, z_there, core))

    for k, dx in enumerate(over_x):
        there = lax.rem(x + dx, NX)
        part = dot_t(gbuf[there, core].reshape(n_z * rows, width), spread[...]).reshape(n_z, rows, 128)
        send_o[there] = part[:, :rows_h] + pltpu.roll(part[:, rows_h:], 64, 2)
        for pair in by_distance:
            if pair[0] == k and far[pair] >= 4:
                put(pair)
    for pair in by_distance:
        if far[pair] < 4:
            put(pair)
    depart()
    arrived(recv_o.at[pl.ds(0, NX * n_z - 1)], o_sem.at[0])
    lower = jnp.zeros((rows_h, 128), F32)
    upper = jnp.zeros((rows_h, 128), F32)
    for k, dx in enumerate(over_x):
        total = send_o[x, z] if dx == 0 else recv_o[k * n_z + n_z - 1]
        for i in range(n_z - 1):
            total = total + recv_o[k * n_z + i]
        source = lax.rem(x + NX - dx, NX)
        lower = lower + jnp.where(source < 2, total, 0.0)
        upper = upper + jnp.where(source < 2, 0.0, total)
    left = lax.broadcasted_iota(jnp.int32, lower.shape, 1) < 64
    o_ref[0:rows_h, :] = jnp.where(left, lower, pltpu.roll(upper, 64, 1))
    o_ref[rows_h:rows, :] = jnp.where(left, pltpu.roll(lower, 64, 1), upper)


def body(n_grp, n_dev, train_grads, query_grads):
    rows, width = train_grads.shape
    block, queries = query_grads.shape
    n_z = n_dev // 4
    ny = n_grp * 2 // NX
    total_rows = rows * n_grp * n_dev
    omega = step_size(width, total_rows)
    slice_q = queries // SLICES
    held = 4 * block
    others_z, others_y = max(n_z - 1, 1), max(ny - 1, 1)
    vmem = pl.BlockSpec(memory_space=pltpu.VMEM)
    anywhere = pl.BlockSpec(memory_space=pl.ANY)
    dma = pltpu.SemaphoreType.DMA
    return pl.pallas_call(
        functools.partial(kernel, n_grp, n_z, omega, total_rows),
        name="influence",
        out_shape=jax.ShapeDtypeStruct((rows, queries), F32),
        in_specs=[anywhere, anywhere],
        out_specs=vmem,
        scratch_shapes=[
            pltpu.VMEM((rows, width), BF16),
            pltpu.VMEM((block, queries), BF16),
            pltpu.VMEM((NX, CORES, n_z, rows, held), BF16),
            pltpu.VMEM((4, block, queries), BF16),
            pltpu.VMEM((queries, held), BF16),
            pltpu.VMEM((n_z, rows, queries), BF16),
            pltpu.VMEM((CORES, n_z, rows, queries), BF16),
            pltpu.VMEM((SLICES * rows, queries), F32),
            pltpu.VMEM((SLICES, slice_q, SLICES * rows), BF16),
            pltpu.VMEM((NX * n_z, slice_q, SLICES * rows), BF16),
            pltpu.VMEM((n_z, slice_q, SLICES * rows), BF16),
            pltpu.VMEM((2, slice_q, SLICES // 2 * n_z * rows), BF16),
            pltpu.VMEM((2, others_z, slice_q, SLICES // 2 * n_z * rows), BF16),
            pltpu.VMEM((ITERS, slice_q, held), BF16),
            pltpu.VMEM((ITERS, others_y, slice_q, held), BF16),
            pltpu.VMEM((ny, slice_q, held), BF16),
            pltpu.VMEM((CORES, slice_q, held), F32),
            pltpu.VMEM((queries, held), BF16),
            pltpu.VMEM((NX, n_z, rows // 2, queries), F32),
            pltpu.VMEM((NX * n_z, rows // 2, queries), F32),
            dma((5,)), dma((1,)), dma((1,)), dma((n_z,)), dma((n_z,)), dma((1,)),
            dma((2,)), pltpu.SemaphoreType.REGULAR, dma((1,)), dma((2,)), dma((ITERS,)), dma((1,)), dma((2,)),
        ],
        compiler_params=pltpu.CompilerParams(
            collective_id=0, has_side_effects=True, vmem_limit_bytes=55168 * 1024
        ),
    )(train_grads, query_grads)


def solution(mesh):
    return jax.shard_map(
        functools.partial(body, mesh.shape["grp"], mesh.shape["dev"]),
        mesh=mesh,
        in_specs=(P(("grp", "dev"), None), P("dev", None)),
        out_specs=P(("grp", "dev"), None),
        check_vma=False,
    )
```

```python
import functools
import math

import jax
import jax.numpy as jnp
from jax import lax
from jax.experimental import pallas as pl
from jax.experimental.pallas import tpu as pltpu
from jax.sharding import PartitionSpec as P

ITERS = 2
DAMP = 1.0
NX = 4
CORES = 2
SLICES = NX * CORES
MESH = pl.DeviceIdType.MESH
F32 = jnp.float32
BF16 = jnp.bfloat16


def step_size(width, total_rows):
    bound = (1.0 + math.sqrt(width / total_rows)) ** 2
    return 1.0 / (1.0 + 1.5 * bound)


def ring(d, n):
    return min(d, n - d)


def farthest_first(n):
    return sorted(range(1, n), key=lambda d: (-ring(d, n), d))


def dot_t(a, b):
    return lax.dot_general(a, b, (((1,), (1,)), ((), ())), preferred_element_type=F32)


def wide(value):
    high = value.astype(BF16)
    return jnp.concatenate([high, (value - high.astype(F32)).astype(BF16)], axis=0)


def folded(value):
    half = value.shape[0] // 2
    return value[:half] + value[half:]


def kernel(
    n_grp, n_z, omega, total_rows,
    g_ref, q_ref, o_ref,
    gl, ql, gbuf, qb, qt, send_f, recv_f, column, sums, recv_e, first, send_s, recv_s, send_t, recv_t, cross_t, swap, spread, send_o, recv_o,
    local_sem, send_sem, q_sem, gz_sem, gx_sem, gc_sem, f_sem, ready_sem, e_sem, s_sem, t_sem, o_sem, w_sem,
):
    rows = g_ref.shape[0]
    block = q_ref.shape[0]
    width = 4 * block
    ny = n_grp * 2 // NX
    grp = lax.axis_index("grp")
    dev = lax.axis_index("dev")
    z, x_lo, core = dev // 4, lax.rem(dev // 2, 2), lax.rem(dev, 2)
    y, x = grp // 2, lax.rem(grp, 2) * 2 + x_lo
    mine = x * CORES + core

    def device(x_at, y_at, z_at, c):
        return (y_at * 2 + x_at // 2, z_at * 4 + lax.rem(x_at, 2) * 2 + c)

    def z_at(d):
        return lax.rem(z + d, n_z)

    along_z = farthest_first(n_z)
    z_partners = [device(x, y, z_at(d), core) for d in along_z]
    z_crossed = [device(x, y, z_at(d), 1 - core) for d in along_z]
    x_partners = [[device(lax.rem(x + d, NX), y, z, c) for c in (core, 1 - core)] for d in farthest_first(NX)]
    y_partners = [device(x, lax.rem(y + d, ny), z, core) for d in farthest_first(ny)]
    sibling = device(x, y, z, 1 - core)
    y_crossed = [device(x, lax.rem(y + d, ny), z, 1 - core) for d in farthest_first(ny)]
    near = device(x + 1 - 2 * x_lo, y, z, core), device(x + 1 - 2 * x_lo, y, z, 1 - core)
    leaving = []

    def push(src, dst, sem, to):
        copy = pltpu.make_async_remote_copy(
            src_ref=src, dst_ref=dst, send_sem=send_sem.at[0], recv_sem=sem, device_id=to, device_id_type=MESH
        )
        copy.start()
        leaving.append(math.prod(src.shape) * src.dtype.itemsize)

    def arrived(like, sem):
        pltpu.make_async_copy(like, like, sem).wait()

    def depart():
        left = sum(leaving)
        leaving.clear()
        for like in (gbuf.at[0], gbuf.at[0, 0, 0], sums.at[0]):
            size = math.prod(like.shape) * like.dtype.itemsize
            while left >= size:
                arrived(like, send_sem.at[0])
                left -= size
        assert left == 0

    def cut(p, n):
        return pl.ds(pl.multiple_of(p * n, n), n)

    load_g = pltpu.make_async_copy(g_ref, gl, local_sem.at[0])
    load_q = pltpu.make_async_copy(q_ref, ql, local_sem.at[1])
    load_g.start()
    load_q.start()

    barrier = pltpu.get_barrier_semaphore()
    partners = z_crossed + z_partners + [same for same, _ in x_partners] + [near[1]] + y_partners + [sibling]
    for to in partners:
        pl.semaphore_signal(barrier, inc=1, device_id=to, device_id_type=MESH)
    pl.semaphore_wait(barrier, len(partners))

    load_g.wait()
    own_g = pltpu.make_async_copy(gl.at[:, cut(z, width)], gbuf.at[x, core, z], local_sem.at[2])
    own_g.start()
    groups = [[0]] + [[d for d in along_z if ring(d, n_z) == far] for far in range(n_z // 2, 0, -1)]
    if len(groups) > 1:
        groups[0] = groups[0] + groups.pop()
    for group in groups:
        for d in group:
            if d:
                push(gl.at[:, cut(z_at(d), width)], gbuf.at[x, core, z], gz_sem.at[n_z - d], device(x, y, z_at(d), core))

    load_q.wait()
    spot = qb.at[x_lo * 2 + core]
    own_q = pltpu.make_async_copy(ql, spot, local_sem.at[3])
    own_q.start()
    for to in (sibling, *near):
        push(ql, spot, q_sem.at[0], to)

    def across(groups):
        for group in groups:
            for d in group:
                arrived(gbuf.at[pl.ds(0, NX - 1), 0, 0], gx_sem.at[d])
                here = gbuf.at[:, core, z_at(d)]
                push(here, here, gc_sem.at[d], sibling)

    own_g.wait()
    for group in groups:
        for d in group:
            here = gbuf.at[x, core, z_at(d)]
            if d:
                arrived(here, gz_sem.at[d])
            for same, _ in x_partners:
                push(here, here, gx_sem.at[d], same)
        if 0 in group:
            own_q.wait()
            arrived(qb.at[pl.ds(0, 3)], q_sem.at[0])
        pieces = [gbuf[x, core, z_at(d)] for d in group]
        pieces = pieces[0] if len(pieces) == 1 else jnp.concatenate(pieces, axis=0)
        part = jnp.dot(pieces, qb[...].reshape(width, qb.shape[-1]), preferred_element_type=F32).astype(BF16)
        for i, d in enumerate(group):
            send_f[d] = part[i * rows : (i + 1) * rows]
            if d:
                push(send_f.at[d], recv_f.at[0, d], f_sem.at[0], device(x, y, z_at(d), core))
                push(send_f.at[d], recv_f.at[1, d], f_sem.at[1], device(x, y, z_at(d), 1 - core))
            else:
                push(send_f.at[d], recv_f.at[1, d], f_sem.at[1], sibling)

    over_x = farthest_first(NX) + [0]
    over_z = along_z + [0]
    far = {(k, i): ring(dx, NX) + ring(dz, n_z) for k, dx in enumerate(over_x) for i, dz in enumerate(over_z)}
    by_distance = sorted((pair for pair in far if far[pair]), key=lambda pair: -far[pair])
    for same, _ in x_partners:
        pl.semaphore_signal(ready_sem, inc=1, device_id=same, device_id_type=MESH)
    qt[...] = qb[...].reshape(width, qb.shape[-1]).astype(F32).T.astype(BF16)
    column[...] = jnp.zeros_like(column)
    spread[...] = jnp.zeros_like(spread)
    across(groups[:2])
    arrived(recv_f.at[1], f_sem.at[1])
    if z_partners:
        arrived(recv_f.at[0, pl.ds(0, n_z - 1)], f_sem.at[0])
    total = send_f[0].astype(F32)
    for d in range(1, n_z):
        total = total + recv_f[0, d].astype(F32)
    column[cut(mine, rows), :] = total
    total = recv_f[1, 0].astype(F32)
    for d in range(1, n_z):
        total = total + recv_f[1, d].astype(F32)
    column[cut(x * CORES + 1 - core, rows), :] = total
    sums[...] = column[...].T.astype(BF16).reshape(sums.shape)
    pl.semaphore_wait(ready_sem, NX - 1)
    for k, i in by_distance:
        there = lax.rem(x + over_x[k], NX)
        to = device(there, y, z_at(over_z[i]), core)
        push(sums.at[there * CORES + core], recv_e.at[k * n_z + i], e_sem.at[0], to)
    across(groups[2:])
    arrived(recv_e.at[pl.ds(0, NX * n_z - 1)], e_sem.at[0])
    for i, dz in enumerate(over_z):
        total = sums[mine] if dz == 0 else recv_e[(NX - 1) * n_z + i]
        for k in range(NX - 1):
            total = total + recv_e[k * n_z + i]
        first[z_at(n_z - dz)] = total
    query = qt[cut(mine, qt.shape[0] // SLICES), :].astype(F32)
    whitened = omega * query
    half_x, slice_q = NX // 2, qt.shape[0] // SLICES
    for sweep in range(ITERS):
        if sweep:
            both = wide(whitened)
            own = []
            for k in (0, 1):
                grads = gbuf[k * half_x : (k + 1) * half_x].reshape(half_x * CORES * n_z * rows, width)
                own.append(folded(dot_t(both, grads)))
                send_s[k] = own[k].astype(BF16)
                for i, to in enumerate(z_partners):
                    push(send_s.at[k], recv_s.at[k, i], s_sem.at[k], to)
            part = jnp.zeros((slice_q, width), F32)
            for k in (0, 1):
                if z_partners:
                    arrived(recv_s.at[k], s_sem.at[k])
                total = own[k]
                for i in range(len(z_partners)):
                    total = total + recv_s[k, i].astype(F32)
                grads = gbuf[k * half_x : (k + 1) * half_x].reshape(half_x * CORES * n_z * rows, width)
                part = part + folded(jnp.dot(wide(total), grads, preferred_element_type=F32))
        else:
            part = jnp.zeros((slice_q, width), F32)
            for some in (groups[:2], groups[2:]):
                there = [z_at(d) for group in some for d in group]
                for group in some:
                    for d in group:
                        arrived(gbuf.at[:, 0, 0], gc_sem.at[d])
                if there:
                    carried = jnp.concatenate([first[at] for at in there], axis=1)
                    grads = [gbuf[:, :, at].reshape(SLICES * rows, width) for at in there]
                    part = part + jnp.dot(carried, jnp.concatenate(grads, axis=0), preferred_element_type=F32)
        send_t[sweep] = part.astype(BF16)
        if sweep == ITERS - 1:
            for i, to in enumerate(y_crossed + [sibling]):
                push(send_t.at[sweep], cross_t.at[i], w_sem.at[1], to)
        for i, to in enumerate(y_partners):
            push(send_t.at[sweep], recv_t.at[sweep, i], t_sem.at[sweep], to)
        if y_partners:
            arrived(recv_t.at[sweep], t_sem.at[sweep])
        total = part
        for i in range(len(y_partners)):
            total = total + recv_t[sweep, i].astype(F32)
        applied = total * (1.0 / total_rows)
        if sweep == 0:
            applied = omega * applied
        whitened = whitened + omega * (query - applied - DAMP * whitened)
        if sweep == ITERS - 2:
            swap[core] = whitened
            push(swap.at[core], swap.at[core], w_sem.at[0], sibling)

    other = x * CORES + 1 - core
    arrived(swap.at[0], w_sem.at[0])
    arrived(cross_t, w_sem.at[1])
    total = cross_t[0].astype(F32)
    for i in range(1, ny):
        total = total + cross_t[i].astype(F32)
    crossed = swap[1 - core]
    query = qt[cut(other, slice_q), :].astype(F32)
    crossed = crossed + omega * (query - total * (1.0 / total_rows) - DAMP * crossed)

    at = lax.rem(x, 2) * CORES
    spread[cut(at + core, slice_q), :] = whitened.astype(BF16)
    spread[cut(at + 1 - core, slice_q), :] = crossed.astype(BF16)
    rows_h = rows // 2

    def put(pair):
        k, i = pair
        there, z_there = lax.rem(x + over_x[k], NX), z_at(over_z[i])
        push(send_o.at[there, z_there], recv_o.at[k * n_z + i], o_sem.at[0], device(there, y, z_there, core))

    for k, dx in enumerate(over_x):
        there = lax.rem(x + dx, NX)
        part = dot_t(gbuf[there, core].reshape(n_z * rows, width), spread[...]).reshape(n_z, rows, 128)
        send_o[there] = part[:, :rows_h] + pltpu.roll(part[:, rows_h:], 64, 2)
        for pair in by_distance:
            if pair[0] == k and far[pair] >= 4:
                put(pair)
    for pair in by_distance:
        if far[pair] < 4:
            put(pair)
    depart()
    arrived(recv_o.at[pl.ds(0, NX * n_z - 1)], o_sem.at[0])
    lower = jnp.zeros((rows_h, 128), F32)
    upper = jnp.zeros((rows_h, 128), F32)
    for k, dx in enumerate(over_x):
        total = send_o[x, z] if dx == 0 else recv_o[k * n_z + n_z - 1]
        for i in range(n_z - 1):
            total = total + recv_o[k * n_z + i]
        source = lax.rem(x + NX - dx, NX)
        lower = lower + jnp.where(source < 2, total, 0.0)
        upper = upper + jnp.where(source < 2, 0.0, total)
    left = lax.broadcasted_iota(jnp.int32, lower.shape, 1) < 64
    o_ref[0:rows_h, :] = jnp.where(left, lower, pltpu.roll(upper, 64, 1))
    o_ref[rows_h:rows, :] = jnp.where(left, pltpu.roll(lower, 64, 1), upper)


def body(n_grp, n_dev, train_grads, query_grads):
    rows, width = train_grads.shape
    block, queries = query_grads.shape
    n_z = n_dev // 4
    ny = n_grp * 2 // NX
    total_rows = rows * n_grp * n_dev
    omega = step_size(width, total_rows)
    slice_q = queries // SLICES
    held = 4 * block
    others_z, others_y = max(n_z - 1, 1), max(ny - 1, 1)
    vmem = pl.BlockSpec(memory_space=pltpu.VMEM)
    anywhere = pl.BlockSpec(memory_space=pl.ANY)
    dma = pltpu.SemaphoreType.DMA
    return pl.pallas_call(
        functools.partial(kernel, n_grp, n_z, omega, total_rows),
        name="influence",
        out_shape=jax.ShapeDtypeStruct((rows, queries), F32),
        in_specs=[anywhere, anywhere],
        out_specs=vmem,
        scratch_shapes=[
            pltpu.VMEM((rows, width), BF16),
            pltpu.VMEM((block, queries), BF16),
            pltpu.VMEM((NX, CORES, n_z, rows, held), BF16),
            pltpu.VMEM((4, block, queries), BF16),
            pltpu.VMEM((queries, held), BF16),
            pltpu.VMEM((n_z, rows, queries), BF16),
            pltpu.VMEM((CORES, n_z, rows, queries), BF16),
            pltpu.VMEM((SLICES * rows, queries), F32),
            pltpu.VMEM((SLICES, slice_q, SLICES * rows), BF16),
            pltpu.VMEM((NX * n_z, slice_q, SLICES * rows), BF16),
            pltpu.VMEM((n_z, slice_q, SLICES * rows), BF16),
            pltpu.VMEM((2, slice_q, SLICES // 2 * n_z * rows), BF16),
            pltpu.VMEM((2, others_z, slice_q, SLICES // 2 * n_z * rows), BF16),
            pltpu.VMEM((ITERS, slice_q, held), BF16),
            pltpu.VMEM((ITERS, others_y, slice_q, held), BF16),
            pltpu.VMEM((ny, slice_q, held), BF16),
            pltpu.VMEM((CORES, slice_q, held), F32),
            pltpu.VMEM((queries, held), BF16),
            pltpu.VMEM((NX, n_z, rows // 2, queries), F32),
            pltpu.VMEM((NX * n_z, rows // 2, queries), F32),
            dma((5,)), dma((1,)), dma((1,)), dma((n_z,)), dma((n_z,)), dma((n_z,)),
            dma((2,)), pltpu.SemaphoreType.REGULAR, dma((1,)), dma((2,)), dma((ITERS,)), dma((1,)), dma((2,)),
        ],
        compiler_params=pltpu.CompilerParams(
            collective_id=0, has_side_effects=True, vmem_limit_bytes=55168 * 1024
        ),
    )(train_grads, query_grads)


def solution(mesh):
    return jax.shard_map(
        functools.partial(body, mesh.shape["grp"], mesh.shape["dev"]),
        mesh=mesh,
        in_specs=(P(("grp", "dev"), None), P("dev", None)),
        out_specs=P(("grp", "dev"), None),
        check_vma=False,
    )
```

```python
import functools
import math

import jax
import jax.numpy as jnp
from jax import lax
from jax.experimental import pallas as pl
from jax.experimental.pallas import tpu as pltpu
from jax.sharding import PartitionSpec as P

ITERS = 2
DAMP = 1.0
NX = 4
CORES = 2
SLICES = NX * CORES
MESH = pl.DeviceIdType.MESH
F32 = jnp.float32
BF16 = jnp.bfloat16


def step_size(width, total_rows):
    bound = (1.0 + math.sqrt(width / total_rows)) ** 2
    return 1.0 / (1.0 + 1.5 * bound)


def ring(d, n):
    return min(d, n - d)


def farthest_first(n):
    return sorted(range(1, n), key=lambda d: (-ring(d, n), d))


def dot_t(a, b):
    return lax.dot_general(a, b, (((1,), (1,)), ((), ())), preferred_element_type=F32)


def wide(value):
    high = value.astype(BF16)
    return jnp.concatenate([high, (value - high.astype(F32)).astype(BF16)], axis=0)


def folded(value):
    half = value.shape[0] // 2
    return value[:half] + value[half:]


def kernel(
    n_grp, n_z, omega, total_rows,
    g_ref, q_ref, o_ref,
    gl, ql, gbuf, qb, qt, send_f, recv_f, column, sums, recv_e, first, send_s, recv_s, send_t, recv_t, cross_t, swap, spread, send_o, recv_o,
    local_sem, send_sem, q_sem, gz_sem, gx_sem, gc_sem, f_sem, ready_sem, e_sem, s_sem, t_sem, o_sem, w_sem,
):
    rows = g_ref.shape[0]
    block = q_ref.shape[0]
    width = 4 * block
    ny = n_grp * 2 // NX
    grp = lax.axis_index("grp")
    dev = lax.axis_index("dev")
    z, x_lo, core = dev // 4, lax.rem(dev // 2, 2), lax.rem(dev, 2)
    y, x = grp // 2, lax.rem(grp, 2) * 2 + x_lo
    mine = x * CORES + core

    def device(x_at, y_at, z_at, c):
        return (y_at * 2 + x_at // 2, z_at * 4 + lax.rem(x_at, 2) * 2 + c)

    def z_at(d):
        return lax.rem(z + d, n_z)

    along_z = farthest_first(n_z)
    z_partners = [device(x, y, z_at(d), core) for d in along_z]
    z_crossed = [device(x, y, z_at(d), 1 - core) for d in along_z]
    x_partners = [[device(lax.rem(x + d, NX), y, z, c) for c in (core, 1 - core)] for d in farthest_first(NX)]
    y_partners = [device(x, lax.rem(y + d, ny), z, core) for d in farthest_first(ny)]
    sibling = device(x, y, z, 1 - core)
    y_crossed = [device(x, lax.rem(y + d, ny), z, 1 - core) for d in farthest_first(ny)]
    near = device(x + 1 - 2 * x_lo, y, z, core)
    leaving = []

    def push(src, dst, sem, to):
        copy = pltpu.make_async_remote_copy(
            src_ref=src, dst_ref=dst, send_sem=send_sem.at[0], recv_sem=sem, device_id=to, device_id_type=MESH
        )
        copy.start()
        leaving.append(math.prod(src.shape) * src.dtype.itemsize)

    def arrived(like, sem):
        pltpu.make_async_copy(like, like, sem).wait()

    def depart():
        left = sum(leaving)
        leaving.clear()
        for like in (gbuf.at[0], gbuf.at[0, 0, 0], sums.at[0]):
            size = math.prod(like.shape) * like.dtype.itemsize
            while left >= size:
                arrived(like, send_sem.at[0])
                left -= size
        assert left == 0

    def cut(p, n):
        return pl.ds(pl.multiple_of(p * n, n), n)

    load_g = pltpu.make_async_copy(g_ref, gl, local_sem.at[0])
    load_q = pltpu.make_async_copy(q_ref, ql, local_sem.at[1])
    load_g.start()
    load_q.start()

    barrier = pltpu.get_barrier_semaphore()
    partners = z_crossed + z_partners + [same for same, _ in x_partners] + y_partners + [sibling]
    for to in partners:
        pl.semaphore_signal(barrier, inc=1, device_id=to, device_id_type=MESH)
    pl.semaphore_wait(barrier, len(partners))

    load_g.wait()
    own_g = pltpu.make_async_copy(gl.at[:, cut(z, width)], gbuf.at[x, core, z], local_sem.at[2])
    own_g.start()
    groups = [[0]] + [[d for d in along_z if ring(d, n_z) == far] for far in range(n_z // 2, 0, -1)]
    if len(groups) > 1:
        groups[0] = groups[0] + groups.pop()
    for group in groups:
        for d in group:
            if d:
                push(gl.at[:, cut(z_at(d), width)], gbuf.at[x, core, z], gz_sem.at[n_z - d], device(x, y, z_at(d), core))

    load_q.wait()
    spot = qb.at[x_lo * 2 + core]
    own_q = pltpu.make_async_copy(ql, spot, local_sem.at[3])
    own_q.start()
    push(ql, spot, q_sem.at[0], near)
    push(ql, spot, q_sem.at[1], sibling)

    def across(groups):
        for group in groups:
            for d in group:
                arrived(gbuf.at[pl.ds(0, NX - 1), 0, 0], gx_sem.at[d])
                here = gbuf.at[:, core, z_at(d)]
                push(here, here, gc_sem.at[d], sibling)

    own_g.wait()
    for group in groups:
        for d in group:
            here = gbuf.at[x, core, z_at(d)]
            if d:
                arrived(here, gz_sem.at[d])
            for same, _ in x_partners:
                push(here, here, gx_sem.at[d], same)
        if 0 in group:
            own_q.wait()
            spot = qb.at[(1 - x_lo) * 2 + core]
            arrived(spot, q_sem.at[0])
            push(spot, spot, q_sem.at[2], sibling)
            arrived(spot, q_sem.at[1])
            arrived(spot, q_sem.at[2])
        pieces = [gbuf[x, core, z_at(d)] for d in group]
        pieces = pieces[0] if len(pieces) == 1 else jnp.concatenate(pieces, axis=0)
        part = jnp.dot(pieces, qb[...].reshape(width, qb.shape[-1]), preferred_element_type=F32).astype(BF16)
        for i, d in enumerate(group):
            send_f[d] = part[i * rows : (i + 1) * rows]
            if d:
                push(send_f.at[d], recv_f.at[0, d], f_sem.at[0], device(x, y, z_at(d), core))
                push(send_f.at[d], recv_f.at[1, d], f_sem.at[1], device(x, y, z_at(d), 1 - core))
            else:
                push(send_f.at[d], recv_f.at[1, d], f_sem.at[1], sibling)

    over_x = farthest_first(NX) + [0]
    over_z = along_z + [0]
    far = {(k, i): ring(dx, NX) + ring(dz, n_z) for k, dx in enumerate(over_x) for i, dz in enumerate(over_z)}
    by_distance = sorted((pair for pair in far if far[pair]), key=lambda pair: -far[pair])
    for same, _ in x_partners:
        pl.semaphore_signal(ready_sem, inc=1, device_id=same, device_id_type=MESH)
    qt[...] = qb[...].reshape(width, qb.shape[-1]).astype(F32).T.astype(BF16)
    column[...] = jnp.zeros_like(column)
    spread[...] = jnp.zeros_like(spread)
    across(groups[:2])
    arrived(recv_f.at[1], f_sem.at[1])
    if z_partners:
        arrived(recv_f.at[0, pl.ds(0, n_z - 1)], f_sem.at[0])
    total = send_f[0].astype(F32)
    for d in range(1, n_z):
        total = total + recv_f[0, d].astype(F32)
    column[cut(mine, rows), :] = total
    total = recv_f[1, 0].astype(F32)
    for d in range(1, n_z):
        total = total + recv_f[1, d].astype(F32)
    column[cut(x * CORES + 1 - core, rows), :] = total
    sums[...] = column[...].T.astype(BF16).reshape(sums.shape)
    pl.semaphore_wait(ready_sem, NX - 1)
    for k, i in by_distance:
        there = lax.rem(x + over_x[k], NX)
        to = device(there, y, z_at(over_z[i]), core)
        push(sums.at[there * CORES + core], recv_e.at[k * n_z + i], e_sem.at[0], to)
    across(groups[2:])
    arrived(recv_e.at[pl.ds(0, NX * n_z - 1)], e_sem.at[0])
    for i, dz in enumerate(over_z):
        total = sums[mine] if dz == 0 else recv_e[(NX - 1) * n_z + i]
        for k in range(NX - 1):
            total = total + recv_e[k * n_z + i]
        first[z_at(n_z - dz)] = total
    query = qt[cut(mine, qt.shape[0] // SLICES), :].astype(F32)
    whitened = omega * query
    half_x, slice_q = NX // 2, qt.shape[0] // SLICES
    for sweep in range(ITERS):
        if sweep:
            both = wide(whitened)
            own = []
            for k in (0, 1):
                grads = gbuf[k * half_x : (k + 1) * half_x].reshape(half_x * CORES * n_z * rows, width)
                own.append(folded(dot_t(both, grads)))
                send_s[k] = own[k].astype(BF16)
                for i, to in enumerate(z_partners):
                    push(send_s.at[k], recv_s.at[k, i], s_sem.at[k], to)
            part = jnp.zeros((slice_q, width), F32)
            for k in (0, 1):
                if z_partners:
                    arrived(recv_s.at[k], s_sem.at[k])
                total = own[k]
                for i in range(len(z_partners)):
                    total = total + recv_s[k, i].astype(F32)
                grads = gbuf[k * half_x : (k + 1) * half_x].reshape(half_x * CORES * n_z * rows, width)
                part = part + folded(jnp.dot(wide(total), grads, preferred_element_type=F32))
        else:
            part = jnp.zeros((slice_q, width), F32)
            for some in (groups[:2], groups[2:]):
                there = [z_at(d) for group in some for d in group]
                for group in some:
                    for d in group:
                        arrived(gbuf.at[:, 0, 0], gc_sem.at[d])
                if there:
                    carried = jnp.concatenate([first[at] for at in there], axis=1)
                    grads = [gbuf[:, :, at].reshape(SLICES * rows, width) for at in there]
                    part = part + jnp.dot(carried, jnp.concatenate(grads, axis=0), preferred_element_type=F32)
        send_t[sweep] = part.astype(BF16)
        if sweep == ITERS - 1:
            for i, to in enumerate(y_crossed + [sibling]):
                push(send_t.at[sweep], cross_t.at[i], w_sem.at[1], to)
        for i, to in enumerate(y_partners):
            push(send_t.at[sweep], recv_t.at[sweep, i], t_sem.at[sweep], to)
        if y_partners:
            arrived(recv_t.at[sweep], t_sem.at[sweep])
        total = part
        for i in range(len(y_partners)):
            total = total + recv_t[sweep, i].astype(F32)
        applied = total * (1.0 / total_rows)
        if sweep == 0:
            applied = omega * applied
        whitened = whitened + omega * (query - applied - DAMP * whitened)
        if sweep == ITERS - 2:
            swap[core] = whitened
            push(swap.at[core], swap.at[core], w_sem.at[0], sibling)

    other = x * CORES + 1 - core
    arrived(swap.at[0], w_sem.at[0])
    arrived(cross_t, w_sem.at[1])
    total = cross_t[0].astype(F32)
    for i in range(1, ny):
        total = total + cross_t[i].astype(F32)
    crossed = swap[1 - core]
    query = qt[cut(other, slice_q), :].astype(F32)
    crossed = crossed + omega * (query - total * (1.0 / total_rows) - DAMP * crossed)

    at = lax.rem(x, 2) * CORES
    spread[cut(at + core, slice_q), :] = whitened.astype(BF16)
    spread[cut(at + 1 - core, slice_q), :] = crossed.astype(BF16)
    rows_h = rows // 2

    def put(pair):
        k, i = pair
        there, z_there = lax.rem(x + over_x[k], NX), z_at(over_z[i])
        push(send_o.at[there, z_there], recv_o.at[k * n_z + i], o_sem.at[0], device(there, y, z_there, core))

    for k, dx in enumerate(over_x):
        there = lax.rem(x + dx, NX)
        part = dot_t(gbuf[there, core].reshape(n_z * rows, width), spread[...]).reshape(n_z, rows, 128)
        send_o[there] = part[:, :rows_h] + pltpu.roll(part[:, rows_h:], 64, 2)
        for pair in by_distance:
            if pair[0] == k and far[pair] >= 4:
                put(pair)
    for pair in by_distance:
        if far[pair] < 4:
            put(pair)
    depart()
    arrived(recv_o.at[pl.ds(0, NX * n_z - 1)], o_sem.at[0])
    lower = jnp.zeros((rows_h, 128), F32)
    upper = jnp.zeros((rows_h, 128), F32)
    for k, dx in enumerate(over_x):
        total = send_o[x, z] if dx == 0 else recv_o[k * n_z + n_z - 1]
        for i in range(n_z - 1):
            total = total + recv_o[k * n_z + i]
        source = lax.rem(x + NX - dx, NX)
        lower = lower + jnp.where(source < 2, total, 0.0)
        upper = upper + jnp.where(source < 2, 0.0, total)
    left = lax.broadcasted_iota(jnp.int32, lower.shape, 1) < 64
    o_ref[0:rows_h, :] = jnp.where(left, lower, pltpu.roll(upper, 64, 1))
    o_ref[rows_h:rows, :] = jnp.where(left, pltpu.roll(lower, 64, 1), upper)


def body(n_grp, n_dev, train_grads, query_grads):
    rows, width = train_grads.shape
    block, queries = query_grads.shape
    n_z = n_dev // 4
    ny = n_grp * 2 // NX
    total_rows = rows * n_grp * n_dev
    omega = step_size(width, total_rows)
    slice_q = queries // SLICES
    held = 4 * block
    others_z, others_y = max(n_z - 1, 1), max(ny - 1, 1)
    vmem = pl.BlockSpec(memory_space=pltpu.VMEM)
    anywhere = pl.BlockSpec(memory_space=pl.ANY)
    dma = pltpu.SemaphoreType.DMA
    return pl.pallas_call(
        functools.partial(kernel, n_grp, n_z, omega, total_rows),
        name="influence",
        out_shape=jax.ShapeDtypeStruct((rows, queries), F32),
        in_specs=[anywhere, anywhere],
        out_specs=vmem,
        scratch_shapes=[
            pltpu.VMEM((rows, width), BF16),
            pltpu.VMEM((block, queries), BF16),
            pltpu.VMEM((NX, CORES, n_z, rows, held), BF16),
            pltpu.VMEM((4, block, queries), BF16),
            pltpu.VMEM((queries, held), BF16),
            pltpu.VMEM((n_z, rows, queries), BF16),
            pltpu.VMEM((CORES, n_z, rows, queries), BF16),
            pltpu.VMEM((SLICES * rows, queries), F32),
            pltpu.VMEM((SLICES, slice_q, SLICES * rows), BF16),
            pltpu.VMEM((NX * n_z, slice_q, SLICES * rows), BF16),
            pltpu.VMEM((n_z, slice_q, SLICES * rows), BF16),
            pltpu.VMEM((2, slice_q, SLICES // 2 * n_z * rows), BF16),
            pltpu.VMEM((2, others_z, slice_q, SLICES // 2 * n_z * rows), BF16),
            pltpu.VMEM((ITERS, slice_q, held), BF16),
            pltpu.VMEM((ITERS, others_y, slice_q, held), BF16),
            pltpu.VMEM((ny, slice_q, held), BF16),
            pltpu.VMEM((CORES, slice_q, held), F32),
            pltpu.VMEM((queries, held), BF16),
            pltpu.VMEM((NX, n_z, rows // 2, queries), F32),
            pltpu.VMEM((NX * n_z, rows // 2, queries), F32),
            dma((5,)), dma((1,)), dma((3,)), dma((n_z,)), dma((n_z,)), dma((n_z,)),
            dma((2,)), pltpu.SemaphoreType.REGULAR, dma((1,)), dma((2,)), dma((ITERS,)), dma((1,)), dma((2,)),
        ],
        compiler_params=pltpu.CompilerParams(
            collective_id=0, has_side_effects=True, vmem_limit_bytes=55168 * 1024
        ),
    )(train_grads, query_grads)


def solution(mesh):
    return jax.shard_map(
        functools.partial(body, mesh.shape["grp"], mesh.shape["dev"]),
        mesh=mesh,
        in_specs=(P(("grp", "dev"), None), P("dev", None)),
        out_specs=P(("grp", "dev"), None),
        check_vma=False,
    )
```

```python
import functools
import math

import jax
import jax.numpy as jnp
from jax import lax
from jax.experimental import pallas as pl
from jax.experimental.pallas import tpu as pltpu
from jax.sharding import PartitionSpec as P

ITERS = 2
DAMP = 1.0
NX = 4
CORES = 2
SLICES = NX * CORES
MESH = pl.DeviceIdType.MESH
F32 = jnp.float32
BF16 = jnp.bfloat16


def step_size(width, total_rows):
    bound = (1.0 + math.sqrt(width / total_rows)) ** 2
    return 1.0 / (1.0 + 1.5 * bound)


def ring(d, n):
    return min(d, n - d)


def farthest_first(n):
    return sorted(range(1, n), key=lambda d: (-ring(d, n), d))


def dot_t(a, b):
    return lax.dot_general(a, b, (((1,), (1,)), ((), ())), preferred_element_type=F32)


def wide(value):
    high = value.astype(BF16)
    return jnp.concatenate([high, (value - high.astype(F32)).astype(BF16)], axis=0)


def folded(value):
    half = value.shape[0] // 2
    return value[:half] + value[half:]


def kernel(
    n_grp, n_z, omega, total_rows,
    g_ref, q_ref, o_ref,
    gl, ql, gbuf, qb, qt, send_f, recv_f, column, sums, recv_e, first, send_s, recv_s, send_t, recv_t, cross_t, swap, spread, send_o, recv_o,
    local_sem, send_sem, q_sem, gz_sem, gx_sem, gc_sem, f_sem, ready_sem, e_sem, s_sem, t_sem, o_sem, w_sem,
):
    rows = g_ref.shape[0]
    block = q_ref.shape[0]
    width = 4 * block
    ny = n_grp * 2 // NX
    grp = lax.axis_index("grp")
    dev = lax.axis_index("dev")
    z, x_lo, core = dev // 4, lax.rem(dev // 2, 2), lax.rem(dev, 2)
    y, x = grp // 2, lax.rem(grp, 2) * 2 + x_lo
    mine = x * CORES + core

    def device(x_at, y_at, z_at, c):
        return (y_at * 2 + x_at // 2, z_at * 4 + lax.rem(x_at, 2) * 2 + c)

    def z_at(d):
        return lax.rem(z + d, n_z)

    along_z = farthest_first(n_z)
    z_partners = [device(x, y, z_at(d), core) for d in along_z]
    z_crossed = [device(x, y, z_at(d), 1 - core) for d in along_z]
    x_partners = [[device(lax.rem(x + d, NX), y, z, c) for c in (core, 1 - core)] for d in farthest_first(NX)]
    y_partners = [device(x, lax.rem(y + d, ny), z, core) for d in farthest_first(ny)]
    sibling = device(x, y, z, 1 - core)
    y_crossed = [device(x, lax.rem(y + d, ny), z, 1 - core) for d in farthest_first(ny)]
    near = device(x + 1 - 2 * x_lo, y, z, core)
    leaving = []

    def push(src, dst, sem, to):
        copy = pltpu.make_async_remote_copy(
            src_ref=src, dst_ref=dst, send_sem=send_sem.at[0], recv_sem=sem, device_id=to, device_id_type=MESH
        )
        copy.start()
        leaving.append(math.prod(src.shape) * src.dtype.itemsize)

    def arrived(like, sem):
        pltpu.make_async_copy(like, like, sem).wait()

    def depart():
        left = sum(leaving)
        leaving.clear()
        for like in (gbuf.at[0], gbuf.at[0, 0, 0], sums.at[0]):
            size = math.prod(like.shape) * like.dtype.itemsize
            while left >= size:
                arrived(like, send_sem.at[0])
                left -= size
        assert left == 0

    def cut(p, n):
        return pl.ds(pl.multiple_of(p * n, n), n)

    load_g = pltpu.make_async_copy(g_ref, gl, local_sem.at[0])
    load_q = pltpu.make_async_copy(q_ref, ql, local_sem.at[1])
    load_g.start()
    load_q.start()

    barrier = pltpu.get_barrier_semaphore()
    partners = z_crossed + z_partners + [same for same, _ in x_partners] + y_partners + [sibling]
    for to in partners:
        pl.semaphore_signal(barrier, inc=1, device_id=to, device_id_type=MESH)
    pl.semaphore_wait(barrier, len(partners))

    load_g.wait()
    own_g = pltpu.make_async_copy(gl.at[:, cut(z, width)], gbuf.at[x, core, z], local_sem.at[2])
    own_g.start()
    groups = [[0]] + [[d for d in along_z if ring(d, n_z) == far] for far in range(n_z // 2, 0, -1)]
    if len(groups) > 1:
        groups[0] = groups[0] + groups.pop()
    for group in groups:
        for d in group:
            if d:
                push(gl.at[:, cut(z_at(d), width)], gbuf.at[x, core, z], gz_sem.at[n_z - d], device(x, y, z_at(d), core))

    load_q.wait()
    spot = qb.at[x_lo * 2 + core]
    own_q = pltpu.make_async_copy(ql, spot, local_sem.at[3])
    own_q.start()
    push(ql, spot, q_sem.at[0], near)
    push(ql, spot, q_sem.at[1], sibling)

    def across(groups):
        for group in groups:
            for d in group:
                arrived(gbuf.at[pl.ds(0, NX - 1), 0, 0], gx_sem.at[d])
                here = gbuf.at[:, core, z_at(d)]
                push(here, here, gc_sem.at[d], sibling)

    own_g.wait()
    for group in groups:
        for d in group:
            here = gbuf.at[x, core, z_at(d)]
            if d:
                arrived(here, gz_sem.at[d])
            for same, _ in x_partners:
                push(here, here, gx_sem.at[d], same)
        if 0 in group:
            own_q.wait()
            spot = qb.at[(1 - x_lo) * 2 + core]
            arrived(spot, q_sem.at[0])
            push(spot, spot, q_sem.at[2], sibling)
            arrived(spot, q_sem.at[1])
            arrived(spot, q_sem.at[2])
        pieces = [gbuf[x, core, z_at(d)] for d in group]
        pieces = pieces[0] if len(pieces) == 1 else jnp.concatenate(pieces, axis=0)
        part = jnp.dot(pieces, qb[...].reshape(width, qb.shape[-1]), preferred_element_type=F32).astype(BF16)
        for i, d in enumerate(group):
            send_f[d] = part[i * rows : (i + 1) * rows]
            if d:
                push(send_f.at[d], recv_f.at[0, d], f_sem.at[0], device(x, y, z_at(d), core))
                push(send_f.at[d], recv_f.at[1, d], f_sem.at[1], device(x, y, z_at(d), 1 - core))
            else:
                push(send_f.at[d], recv_f.at[1, d], f_sem.at[1], sibling)

    over_x = farthest_first(NX) + [0]
    over_z = along_z + [0]
    far = {(k, i): ring(dx, NX) + ring(dz, n_z) for k, dx in enumerate(over_x) for i, dz in enumerate(over_z)}
    by_distance = sorted((pair for pair in far if far[pair]), key=lambda pair: -far[pair])
    for same, _ in x_partners:
        pl.semaphore_signal(ready_sem, inc=1, device_id=same, device_id_type=MESH)
    qt[...] = qb[...].reshape(width, qb.shape[-1]).astype(F32).T.astype(BF16)
    column[...] = jnp.zeros_like(column)
    spread[...] = jnp.zeros_like(spread)
    across(groups[:2])
    arrived(recv_f.at[1], f_sem.at[1])
    if z_partners:
        arrived(recv_f.at[0, pl.ds(0, n_z - 1)], f_sem.at[0])
    total = send_f[0].astype(F32)
    for d in range(1, n_z):
        total = total + recv_f[0, d].astype(F32)
    column[cut(mine, rows), :] = total
    total = recv_f[1, 0].astype(F32)
    for d in range(1, n_z):
        total = total + recv_f[1, d].astype(F32)
    column[cut(x * CORES + 1 - core, rows), :] = total
    sums[...] = column[...].T.astype(BF16).reshape(sums.shape)
    pl.semaphore_wait(ready_sem, NX - 1)
    for k, i in by_distance:
        there = lax.rem(x + over_x[k], NX)
        to = device(there, y, z_at(over_z[i]), core)
        push(sums.at[there * CORES + core], recv_e.at[k * n_z + i], e_sem.at[0], to)
    across(groups[2:])
    arrived(recv_e.at[pl.ds(0, NX * n_z - 1)], e_sem.at[0])
    for i, dz in enumerate(over_z):
        total = sums[mine] if dz == 0 else recv_e[(NX - 1) * n_z + i]
        for k in range(NX - 1):
            total = total + recv_e[k * n_z + i]
        first[z_at(n_z - dz)] = total
    query = qt[cut(mine, qt.shape[0] // SLICES), :].astype(F32)
    whitened = omega * query
    half_x, slice_q = NX // 2, qt.shape[0] // SLICES
    for sweep in range(ITERS):
        if sweep:
            both = wide(whitened)
            own = []
            for k in (0, 1):
                grads = gbuf[k * half_x : (k + 1) * half_x].reshape(half_x * CORES * n_z * rows, width)
                own.append(folded(dot_t(both, grads)))
                send_s[k] = own[k].astype(BF16)
                for i, to in enumerate(z_partners):
                    push(send_s.at[k], recv_s.at[k, i], s_sem.at[k], to)
            swap[core] = whitened
            push(swap.at[core], swap.at[core], w_sem.at[0], sibling)
            part = jnp.zeros((slice_q, width), F32)
            for k in (0, 1):
                if z_partners:
                    arrived(recv_s.at[k], s_sem.at[k])
                total = own[k]
                for i in range(len(z_partners)):
                    total = total + recv_s[k, i].astype(F32)
                grads = gbuf[k * half_x : (k + 1) * half_x].reshape(half_x * CORES * n_z * rows, width)
                part = part + folded(jnp.dot(wide(total), grads, preferred_element_type=F32))
        else:
            part = jnp.zeros((slice_q, width), F32)
            for some in (groups[:2], groups[2:3], groups[3:]):
                there = [z_at(d) for group in some for d in group]
                for group in some:
                    for d in group:
                        arrived(gbuf.at[:, 0, 0], gc_sem.at[d])
                if there:
                    carried = jnp.concatenate([first[at] for at in there], axis=1)
                    grads = [gbuf[:, :, at].reshape(SLICES * rows, width) for at in there]
                    part = part + jnp.dot(carried, jnp.concatenate(grads, axis=0), preferred_element_type=F32)
        send_t[sweep] = part.astype(BF16)
        if sweep == ITERS - 1:
            for i, to in enumerate(y_crossed + [sibling]):
                push(send_t.at[sweep], cross_t.at[i], w_sem.at[1], to)
        for i, to in enumerate(y_partners):
            push(send_t.at[sweep], recv_t.at[sweep, i], t_sem.at[sweep], to)
        if y_partners:
            arrived(recv_t.at[sweep], t_sem.at[sweep])
        total = part
        for i in range(len(y_partners)):
            total = total + recv_t[sweep, i].astype(F32)
        applied = total * (1.0 / total_rows)
        if sweep == 0:
            applied = omega * applied
        whitened = whitened + omega * (query - applied - DAMP * whitened)

    other = x * CORES + 1 - core
    arrived(swap.at[0], w_sem.at[0])
    arrived(cross_t, w_sem.at[1])
    total = cross_t[0].astype(F32)
    for i in range(1, ny):
        total = total + cross_t[i].astype(F32)
    crossed = swap[1 - core]
    query = qt[cut(other, slice_q), :].astype(F32)
    crossed = crossed + omega * (query - total * (1.0 / total_rows) - DAMP * crossed)

    at = lax.rem(x, 2) * CORES
    spread[cut(at + core, slice_q), :] = whitened.astype(BF16)
    spread[cut(at + 1 - core, slice_q), :] = crossed.astype(BF16)
    rows_h = rows // 2

    def put(pair):
        k, i = pair
        there, z_there = lax.rem(x + over_x[k], NX), z_at(over_z[i])
        push(send_o.at[there, z_there], recv_o.at[k * n_z + i], o_sem.at[0], device(there, y, z_there, core))

    for k, dx in enumerate(over_x):
        there = lax.rem(x + dx, NX)
        part = dot_t(gbuf[there, core].reshape(n_z * rows, width), spread[...]).reshape(n_z, rows, 128)
        send_o[there] = part[:, :rows_h] + pltpu.roll(part[:, rows_h:], 64, 2)
        for pair in by_distance:
            if pair[0] == k and far[pair] >= 4:
                put(pair)
    for pair in by_distance:
        if far[pair] < 4:
            put(pair)
    depart()
    arrived(recv_o.at[pl.ds(0, NX * n_z - 1)], o_sem.at[0])
    lower = jnp.zeros((rows_h, 128), F32)
    upper = jnp.zeros((rows_h, 128), F32)
    for k, dx in enumerate(over_x):
        total = send_o[x, z] if dx == 0 else recv_o[k * n_z + n_z - 1]
        for i in range(n_z - 1):
            total = total + recv_o[k * n_z + i]
        source = lax.rem(x + NX - dx, NX)
        lower = lower + jnp.where(source < 2, total, 0.0)
        upper = upper + jnp.where(source < 2, 0.0, total)
    left = lax.broadcasted_iota(jnp.int32, lower.shape, 1) < 64
    o_ref[0:rows_h, :] = jnp.where(left, lower, pltpu.roll(upper, 64, 1))
    o_ref[rows_h:rows, :] = jnp.where(left, pltpu.roll(lower, 64, 1), upper)


def body(n_grp, n_dev, train_grads, query_grads):
    rows, width = train_grads.shape
    block, queries = query_grads.shape
    n_z = n_dev // 4
    ny = n_grp * 2 // NX
    total_rows = rows * n_grp * n_dev
    omega = step_size(width, total_rows)
    slice_q = queries // SLICES
    held = 4 * block
    others_z, others_y = max(n_z - 1, 1), max(ny - 1, 1)
    vmem = pl.BlockSpec(memory_space=pltpu.VMEM)
    anywhere = pl.BlockSpec(memory_space=pl.ANY)
    dma = pltpu.SemaphoreType.DMA
    return pl.pallas_call(
        functools.partial(kernel, n_grp, n_z, omega, total_rows),
        name="influence",
        out_shape=jax.ShapeDtypeStruct((rows, queries), F32),
        in_specs=[anywhere, anywhere],
        out_specs=vmem,
        scratch_shapes=[
            pltpu.VMEM((rows, width), BF16),
            pltpu.VMEM((block, queries), BF16),
            pltpu.VMEM((NX, CORES, n_z, rows, held), BF16),
            pltpu.VMEM((4, block, queries), BF16),
            pltpu.VMEM((queries, held), BF16),
            pltpu.VMEM((n_z, rows, queries), BF16),
            pltpu.VMEM((CORES, n_z, rows, queries), BF16),
            pltpu.VMEM((SLICES * rows, queries), F32),
            pltpu.VMEM((SLICES, slice_q, SLICES * rows), BF16),
            pltpu.VMEM((NX * n_z, slice_q, SLICES * rows), BF16),
            pltpu.VMEM((n_z, slice_q, SLICES * rows), BF16),
            pltpu.VMEM((2, slice_q, SLICES // 2 * n_z * rows), BF16),
            pltpu.VMEM((2, others_z, slice_q, SLICES // 2 * n_z * rows), BF16),
            pltpu.VMEM((ITERS, slice_q, held), BF16),
            pltpu.VMEM((ITERS, others_y, slice_q, held), BF16),
            pltpu.VMEM((ny, slice_q, held), BF16),
            pltpu.VMEM((CORES, slice_q, held), F32),
            pltpu.VMEM((queries, held), BF16),
            pltpu.VMEM((NX, n_z, rows // 2, queries), F32),
            pltpu.VMEM((NX * n_z, rows // 2, queries), F32),
            dma((5,)), dma((1,)), dma((3,)), dma((n_z,)), dma((n_z,)), dma((n_z,)),
            dma((2,)), pltpu.SemaphoreType.REGULAR, dma((1,)), dma((2,)), dma((ITERS,)), dma((1,)), dma((2,)),
        ],
        compiler_params=pltpu.CompilerParams(
            collective_id=0, has_side_effects=True, vmem_limit_bytes=55168 * 1024
        ),
    )(train_grads, query_grads)


def solution(mesh):
    return jax.shard_map(
        functools.partial(body, mesh.shape["grp"], mesh.shape["dev"]),
        mesh=mesh,
        in_specs=(P(("grp", "dev"), None), P("dev", None)),
        out_specs=P(("grp", "dev"), None),
        check_vma=False,
    )
```

```python
import functools
import math

import jax
import jax.numpy as jnp
from jax import lax
from jax.experimental import pallas as pl
from jax.experimental.pallas import tpu as pltpu
from jax.sharding import PartitionSpec as P

ITERS = 2
DAMP = 1.0
NX = 4
CORES = 2
SLICES = NX * CORES
MESH = pl.DeviceIdType.MESH
F32 = jnp.float32
BF16 = jnp.bfloat16


def step_size(width, total_rows):
    bound = (1.0 + math.sqrt(width / total_rows)) ** 2
    return 1.0 / (1.0 + 1.5 * bound)


def ring(d, n):
    return min(d, n - d)


def farthest_first(n):
    return sorted(range(1, n), key=lambda d: (-ring(d, n), d))


def dot_t(a, b):
    return lax.dot_general(a, b, (((1,), (1,)), ((), ())), preferred_element_type=F32)


def wide(value):
    high = value.astype(BF16)
    return jnp.concatenate([high, (value - high.astype(F32)).astype(BF16)], axis=0)


def folded(value):
    half = value.shape[0] // 2
    return value[:half] + value[half:]


def kernel(
    n_grp, n_z, omega, total_rows,
    g_ref, q_ref, o_ref,
    gl, ql, gbuf, qb, qt, send_f, recv_f, column, sums, recv_e, first, send_s, recv_s, send_t, recv_t, cross_t, swap, spread, send_o, recv_o,
    local_sem, send_sem, q_sem, gz_sem, gx_sem, gc_sem, f_sem, ready_sem, e_sem, s_sem, t_sem, o_sem, w_sem,
):
    rows = g_ref.shape[0]
    block = q_ref.shape[0]
    width = 4 * block
    ny = n_grp * 2 // NX
    grp = lax.axis_index("grp")
    dev = lax.axis_index("dev")
    z, x_lo, core = dev // 4, lax.rem(dev // 2, 2), lax.rem(dev, 2)
    y, x = grp // 2, lax.rem(grp, 2) * 2 + x_lo
    mine = x * CORES + core

    def device(x_at, y_at, z_at, c):
        return (y_at * 2 + x_at // 2, z_at * 4 + lax.rem(x_at, 2) * 2 + c)

    def z_at(d):
        return lax.rem(z + d, n_z)

    along_z = farthest_first(n_z)
    z_partners = [device(x, y, z_at(d), core) for d in along_z]
    z_crossed = [device(x, y, z_at(d), 1 - core) for d in along_z]
    x_partners = [[device(lax.rem(x + d, NX), y, z, c) for c in (core, 1 - core)] for d in farthest_first(NX)]
    y_partners = [device(x, lax.rem(y + d, ny), z, core) for d in farthest_first(ny)]
    sibling = device(x, y, z, 1 - core)
    y_crossed = [device(x, lax.rem(y + d, ny), z, 1 - core) for d in farthest_first(ny)]
    near = device(x + 1 - 2 * x_lo, y, z, core)
    leaving = []

    def push(src, dst, sem, to):
        copy = pltpu.make_async_remote_copy(
            src_ref=src, dst_ref=dst, send_sem=send_sem.at[0], recv_sem=sem, device_id=to, device_id_type=MESH
        )
        copy.start()
        leaving.append(math.prod(src.shape) * src.dtype.itemsize)

    def arrived(like, sem):
        pltpu.make_async_copy(like, like, sem).wait()

    def depart():
        left = sum(leaving)
        leaving.clear()
        for like in (gbuf.at[0], gbuf.at[0, 0, 0], sums.at[0]):
            size = math.prod(like.shape) * like.dtype.itemsize
            while left >= size:
                arrived(like, send_sem.at[0])
                left -= size
        assert left == 0

    def cut(p, n):
        return pl.ds(pl.multiple_of(p * n, n), n)

    load_g = pltpu.make_async_copy(g_ref, gl, local_sem.at[0])
    load_q = pltpu.make_async_copy(q_ref, ql, local_sem.at[1])
    load_g.start()
    load_q.start()

    barrier = pltpu.get_barrier_semaphore()
    partners = z_crossed + z_partners + [same for same, _ in x_partners] + y_partners + [sibling]
    for to in partners:
        pl.semaphore_signal(barrier, inc=1, device_id=to, device_id_type=MESH)
    pl.semaphore_wait(barrier, len(partners))

    load_g.wait()
    own_g = pltpu.make_async_copy(gl.at[:, cut(z, width)], gbuf.at[x, core, z], local_sem.at[2])
    own_g.start()
    groups = [[0]] + [[d for d in along_z if ring(d, n_z) == far] for far in range(n_z // 2, 0, -1)]
    if len(groups) > 1:
        groups[0] = groups[0] + groups.pop()
    for group in groups:
        for d in group:
            if d:
                push(gl.at[:, cut(z_at(d), width)], gbuf.at[x, core, z], gz_sem.at[n_z - d], device(x, y, z_at(d), core))

    load_q.wait()
    spot = qb.at[x_lo * 2 + core]
    own_q = pltpu.make_async_copy(ql, spot, local_sem.at[3])
    own_q.start()
    push(ql, spot, q_sem.at[0], near)
    push(ql, spot, q_sem.at[1], sibling)

    def across(groups):
        for group in groups:
            for d in group:
                arrived(gbuf.at[pl.ds(0, NX - 1), 0, 0], gx_sem.at[d])
                here = gbuf.at[:, core, z_at(d)]
                push(here, here, gc_sem.at[d], sibling)

    for group in groups:
        for d in group:
            here = gbuf.at[x, core, z_at(d)]
            if d:
                arrived(here, gz_sem.at[d])
            for same, _ in x_partners:
                push(here if d else gl.at[:, cut(z, width)], here, gx_sem.at[d], same)
        if 0 in group:
            own_g.wait()
            own_q.wait()
            spot = qb.at[(1 - x_lo) * 2 + core]
            arrived(spot, q_sem.at[0])
            push(spot, spot, q_sem.at[2], sibling)
            arrived(spot, q_sem.at[1])
            arrived(spot, q_sem.at[2])
        pieces = [gbuf[x, core, z_at(d)] for d in group]
        pieces = pieces[0] if len(pieces) == 1 else jnp.concatenate(pieces, axis=0)
        part = jnp.dot(pieces, qb[...].reshape(width, qb.shape[-1]), preferred_element_type=F32).astype(BF16)
        for i, d in enumerate(group):
            send_f[d] = part[i * rows : (i + 1) * rows]
            if d:
                push(send_f.at[d], recv_f.at[0, d], f_sem.at[0], device(x, y, z_at(d), core))
                push(send_f.at[d], recv_f.at[1, d], f_sem.at[1], device(x, y, z_at(d), 1 - core))
            else:
                push(send_f.at[d], recv_f.at[1, d], f_sem.at[1], sibling)

    over_x = farthest_first(NX) + [0]
    over_z = along_z + [0]
    far = {(k, i): ring(dx, NX) + ring(dz, n_z) for k, dx in enumerate(over_x) for i, dz in enumerate(over_z)}
    by_distance = sorted((pair for pair in far if far[pair]), key=lambda pair: -far[pair])
    for same, _ in x_partners:
        pl.semaphore_signal(ready_sem, inc=1, device_id=same, device_id_type=MESH)
    qt[...] = qb[...].reshape(width, qb.shape[-1]).astype(F32).T.astype(BF16)
    column[...] = jnp.zeros_like(column)
    spread[...] = jnp.zeros_like(spread)
    across(groups[:2])
    arrived(recv_f.at[1], f_sem.at[1])
    if z_partners:
        arrived(recv_f.at[0, pl.ds(0, n_z - 1)], f_sem.at[0])
    total = send_f[0].astype(F32)
    for d in range(1, n_z):
        total = total + recv_f[0, d].astype(F32)
    column[cut(mine, rows), :] = total
    total = recv_f[1, 0].astype(F32)
    for d in range(1, n_z):
        total = total + recv_f[1, d].astype(F32)
    column[cut(x * CORES + 1 - core, rows), :] = total
    sums[...] = column[...].T.astype(BF16).reshape(sums.shape)
    pl.semaphore_wait(ready_sem, NX - 1)
    for k, i in by_distance:
        there = lax.rem(x + over_x[k], NX)
        to = device(there, y, z_at(over_z[i]), core)
        push(sums.at[there * CORES + core], recv_e.at[k * n_z + i], e_sem.at[0], to)
    across(groups[2:])
    arrived(recv_e.at[pl.ds(0, NX * n_z - 1)], e_sem.at[0])
    for i, dz in enumerate(over_z):
        total = sums[mine] if dz == 0 else recv_e[(NX - 1) * n_z + i]
        for k in range(NX - 1):
            total = total + recv_e[k * n_z + i]
        first[z_at(n_z - dz)] = total
    query = qt[cut(mine, qt.shape[0] // SLICES), :].astype(F32)
    whitened = omega * query
    half_x, slice_q = NX // 2, qt.shape[0] // SLICES
    for sweep in range(ITERS):
        if sweep:
            both = wide(whitened)
            own = []
            for k in (0, 1):
                grads = gbuf[k * half_x : (k + 1) * half_x].reshape(half_x * CORES * n_z * rows, width)
                own.append(folded(dot_t(both, grads)))
                send_s[k] = own[k].astype(BF16)
                for i, to in enumerate(z_partners):
                    push(send_s.at[k], recv_s.at[k, i], s_sem.at[k], to)
            swap[core] = whitened
            push(swap.at[core], swap.at[core], w_sem.at[0], sibling)
            part = jnp.zeros((slice_q, width), F32)
            for k in (0, 1):
                if z_partners:
                    arrived(recv_s.at[k], s_sem.at[k])
                total = own[k]
                for i in range(len(z_partners)):
                    total = total + recv_s[k, i].astype(F32)
                grads = gbuf[k * half_x : (k + 1) * half_x].reshape(half_x * CORES * n_z * rows, width)
                part = part + folded(jnp.dot(wide(total), grads, preferred_element_type=F32))
        else:
            part = jnp.zeros((slice_q, width), F32)
            for some in (groups[:2], groups[2:3], groups[3:]):
                there = [z_at(d) for group in some for d in group]
                for group in some:
                    for d in group:
                        arrived(gbuf.at[:, 0, 0], gc_sem.at[d])
                if there:
                    carried = jnp.concatenate([first[at] for at in there], axis=1)
                    grads = [gbuf[:, :, at].reshape(SLICES * rows, width) for at in there]
                    part = part + jnp.dot(carried, jnp.concatenate(grads, axis=0), preferred_element_type=F32)
        send_t[sweep] = part.astype(BF16)
        if sweep == ITERS - 1:
            for i, to in enumerate(y_crossed + [sibling]):
                push(send_t.at[sweep], cross_t.at[i], w_sem.at[1], to)
        for i, to in enumerate(y_partners):
            push(send_t.at[sweep], recv_t.at[sweep, i], t_sem.at[sweep], to)
        if y_partners:
            arrived(recv_t.at[sweep], t_sem.at[sweep])
        total = part
        for i in range(len(y_partners)):
            total = total + recv_t[sweep, i].astype(F32)
        applied = total * (1.0 / total_rows)
        if sweep == 0:
            applied = omega * applied
        whitened = whitened + omega * (query - applied - DAMP * whitened)

    other = x * CORES + 1 - core
    arrived(swap.at[0], w_sem.at[0])
    arrived(cross_t, w_sem.at[1])
    total = cross_t[0].astype(F32)
    for i in range(1, ny):
        total = total + cross_t[i].astype(F32)
    crossed = swap[1 - core]
    query = qt[cut(other, slice_q), :].astype(F32)
    crossed = crossed + omega * (query - total * (1.0 / total_rows) - DAMP * crossed)

    at = lax.rem(x, 2) * CORES
    spread[cut(at + core, slice_q), :] = whitened.astype(BF16)
    spread[cut(at + 1 - core, slice_q), :] = crossed.astype(BF16)
    rows_h = rows // 2

    def put(pair):
        k, i = pair
        there, z_there = lax.rem(x + over_x[k], NX), z_at(over_z[i])
        push(send_o.at[there, z_there], recv_o.at[k * n_z + i], o_sem.at[0], device(there, y, z_there, core))

    for k, dx in enumerate(over_x):
        there = lax.rem(x + dx, NX)
        part = dot_t(gbuf[there, core].reshape(n_z * rows, width), spread[...]).reshape(n_z, rows, 128)
        send_o[there] = part[:, :rows_h] + pltpu.roll(part[:, rows_h:], 64, 2)
        for pair in by_distance:
            if pair[0] == k and far[pair] >= 4:
                put(pair)
    for pair in by_distance:
        if far[pair] < 4:
            put(pair)
    depart()
    arrived(recv_o.at[pl.ds(0, NX * n_z - 1)], o_sem.at[0])
    lower = jnp.zeros((rows_h, 128), F32)
    upper = jnp.zeros((rows_h, 128), F32)
    for k, dx in enumerate(over_x):
        total = send_o[x, z] if dx == 0 else recv_o[k * n_z + n_z - 1]
        for i in range(n_z - 1):
            total = total + recv_o[k * n_z + i]
        source = lax.rem(x + NX - dx, NX)
        lower = lower + jnp.where(source < 2, total, 0.0)
        upper = upper + jnp.where(source < 2, 0.0, total)
    left = lax.broadcasted_iota(jnp.int32, lower.shape, 1) < 64
    o_ref[0:rows_h, :] = jnp.where(left, lower, pltpu.roll(upper, 64, 1))
    o_ref[rows_h:rows, :] = jnp.where(left, pltpu.roll(lower, 64, 1), upper)


def body(n_grp, n_dev, train_grads, query_grads):
    rows, width = train_grads.shape
    block, queries = query_grads.shape
    n_z = n_dev // 4
    ny = n_grp * 2 // NX
    total_rows = rows * n_grp * n_dev
    omega = step_size(width, total_rows)
    slice_q = queries // SLICES
    held = 4 * block
    others_z, others_y = max(n_z - 1, 1), max(ny - 1, 1)
    vmem = pl.BlockSpec(memory_space=pltpu.VMEM)
    anywhere = pl.BlockSpec(memory_space=pl.ANY)
    dma = pltpu.SemaphoreType.DMA
    return pl.pallas_call(
        functools.partial(kernel, n_grp, n_z, omega, total_rows),
        name="influence",
        out_shape=jax.ShapeDtypeStruct((rows, queries), F32),
        in_specs=[anywhere, anywhere],
        out_specs=vmem,
        scratch_shapes=[
            pltpu.VMEM((rows, width), BF16),
            pltpu.VMEM((block, queries), BF16),
            pltpu.VMEM((NX, CORES, n_z, rows, held), BF16),
            pltpu.VMEM((4, block, queries), BF16),
            pltpu.VMEM((queries, held), BF16),
            pltpu.VMEM((n_z, rows, queries), BF16),
            pltpu.VMEM((CORES, n_z, rows, queries), BF16),
            pltpu.VMEM((SLICES * rows, queries), F32),
            pltpu.VMEM((SLICES, slice_q, SLICES * rows), BF16),
            pltpu.VMEM((NX * n_z, slice_q, SLICES * rows), BF16),
            pltpu.VMEM((n_z, slice_q, SLICES * rows), BF16),
            pltpu.VMEM((2, slice_q, SLICES // 2 * n_z * rows), BF16),
            pltpu.VMEM((2, others_z, slice_q, SLICES // 2 * n_z * rows), BF16),
            pltpu.VMEM((ITERS, slice_q, held), BF16),
            pltpu.VMEM((ITERS, others_y, slice_q, held), BF16),
            pltpu.VMEM((ny, slice_q, held), BF16),
            pltpu.VMEM((CORES, slice_q, held), F32),
            pltpu.VMEM((queries, held), BF16),
            pltpu.VMEM((NX, n_z, rows // 2, queries), F32),
            pltpu.VMEM((NX * n_z, rows // 2, queries), F32),
            dma((5,)), dma((1,)), dma((3,)), dma((n_z,)), dma((n_z,)), dma((n_z,)),
            dma((2,)), pltpu.SemaphoreType.REGULAR, dma((1,)), dma((2,)), dma((ITERS,)), dma((1,)), dma((2,)),
        ],
        compiler_params=pltpu.CompilerParams(
            collective_id=0, has_side_effects=True, vmem_limit_bytes=55168 * 1024
        ),
    )(train_grads, query_grads)


def solution(mesh):
    return jax.shard_map(
        functools.partial(body, mesh.shape["grp"], mesh.shape["dev"]),
        mesh=mesh,
        in_specs=(P(("grp", "dev"), None), P("dev", None)),
        out_specs=P(("grp", "dev"), None),
        check_vma=False,
    )
```
